512 devices in a mesh: dom: 128 (over x, z, core), sub: 4 (over y).
Axes of the slice: x: 4, y: 4, z: 16, core: 2. Of those that a mesh axis runs over, the one named last changes fastest.
Arguments:
- features: bfloat16 [524288, 256], P(('dom', 'sub')), may hold values from -16 to 16
- weight: bfloat16 [256, 256], replicated, may hold values from -0.375 to 0.375
- send_far: int32 [262144], P(('dom', 'sub')), may hold values from 0 to 1023
- send_near: int32 [65536], P(('dom', 'sub')), may hold values from 0 to 1023
- tile_dst: int32 [8192], P(('dom', 'sub')), may hold values from 0 to 7
- inner_src: int32 [4096], P(('dom', 'sub')), may hold values from 0 to 7
- outer_src: int32 [4096], P(('dom', 'sub')), may hold values from 0 to 4
- tile_live: int32 [512, 2], P(('dom', 'sub')), may hold values from 4 to 8
- tile_weight: bfloat16 [8192, 128, 128], P(('dom', 'sub')), may hold values from -0.3125 to 0.3125
Outputs:
- whitened: bfloat16 [524288, 256], P(('dom', 'sub'))
- loss_value: float32 [], replicated
The draws below stay inside these ranges and needn't reach their ends.
Inputs may be any that keep to these rules, and one draw needn't show every extreme that they name: `send_far`: rows may repeat. `tile_live`: live slots come first in each half of a device's slots.
All inputs are finite; a program needn't handle non-finite values.
Results may differ from the reference program's by a relative error of at most 0.0085.
Values may be sent and summed in bfloat16 or wider, within the bound.
No kernel may reach another device: no remote copies, remote signals or barrier semaphores. Data moves between devices by JAX's collectives and lax.ppermute only.
A program may use at most 64 MiB of HBM per device.

```python
import jax
import jax.numpy as jnp
from jax import lax

F = 256
B = 128
V_DEV = 1024
HALO_DOM = 512
SLOTS = 8
HALO_SUB = 128
PEER_DOM = 4
PEER_SUB = 32
VERTS = 524288
N_DOM = 128
N_SUB = 4


def draw_features(key, part):
    key_base = jax.random.fold_in(key, 11)
    key_jitter = jax.random.fold_in(key, 14)
    key_shift = jax.random.fold_in(key, 15)
    key_heavy = jax.random.fold_in(key, 16)
    key_sign = jax.random.fold_in(key, 17)
    block_count = VERTS // V_DEV
    block_index = jnp.arange(block_count, dtype=jnp.int32)
    sub_place = (block_index % N_SUB).astype(jnp.float32) / max(N_SUB - 1, 1)
    dom_place = (block_index // N_SUB).astype(jnp.float32) / max(block_count // N_SUB - 1, 1)
    jitter = jax.random.uniform(key_jitter, (block_count,), jnp.float32, -0.3, 0.3)
    block_scale = jnp.exp(-0.6 + 0.6 * sub_place + 0.5 * dom_place + jitter)
    block_shift = jax.random.uniform(key_shift, (block_count, 1, F), jnp.float32, -0.5, 0.5)
    array_shape = (block_count, V_DEV, F)
    base_values = jnp.clip(jax.random.normal(key_base, array_shape, jnp.float32), -6.0, 6.0)
    values = base_values * block_scale[:, None, None] + block_shift
    values = jnp.clip(values, -9.0, 9.0)
    heavy_noise = jnp.clip(jax.random.normal(key_heavy, (block_count, V_DEV, 1), jnp.float32), -2.5, 2.5)
    block_sign = jnp.where(jax.random.bernoulli(key_sign, 0.5, (block_count, 1, 1)), 1.0, -1.0).astype(jnp.float32)
    heavy_values = block_sign * (12.0 + 1.5 * heavy_noise)
    column_index = jnp.arange(F, dtype=jnp.int32)
    heavy_mask = column_index[None, None, :] == (block_index % F)[:, None, None]
    values = jnp.where(heavy_mask, heavy_values, values)
    values = jnp.clip(values, -16.0, 16.0).reshape(VERTS, F)
    return values.astype(jnp.bfloat16)


def plant(entries, own_key, least, top_value):
    longest = entries.shape.index(max(entries.shape))
    spots = []
    for shift in (0, 1):
        where = [jax.random.randint(jax.random.fold_in(own_key, axis), (), 0, length) for axis, length in enumerate(entries.shape)]
        where[longest] = (where[longest] + shift) % entries.shape[longest]
        spots.append(tuple(where))
    return entries.at[spots[0]].set(least).at[spots[1]].set(top_value)


def steps_of(stream_key, shape, cuts, low, top_value):
    def one(dim, parts):
        heights = jax.random.uniform(jax.random.fold_in(jax.random.fold_in(stream_key, 6), dim), (parts,), jnp.float32, low / len(cuts), top_value / len(cuts))
        return jnp.repeat(jnp.exp(heights), shape[dim] // parts).reshape((-1,) + (1,) * (len(shape) - dim - 1))

    loudness = one(*cuts[0])
    for cut in cuts[1:]:
        loudness = loudness * one(*cut)
    return loudness


def normal_values(key, extent, deviation, limit, pieces=(), kind=jnp.bfloat16):
    level = steps_of(key, extent, pieces, -0.22, 0.18) if pieces else 1.0
    result = jax.random.normal(key, extent, jnp.float32) * deviation * level
    return jnp.minimum(jnp.maximum(result, -limit), limit).astype(kind)


def setup_inputs(seed: int = 0) -> dict:
    key_of = jax.random.split(jax.random.key(seed), 10)
    return {
        "features": draw_features(jax.random.fold_in(key_of[9], 71), 0),
        "weight": normal_values(key_of[1], (F, F), F ** -0.5, 0.375),
        "send_far": plant(jax.random.randint(key_of[2], (N_DOM * N_SUB * HALO_DOM,), 0, V_DEV), jax.random.fold_in(key_of[2], 1), 0, V_DEV - 1).astype(jnp.int32),
        "send_near": plant(jax.random.randint(key_of[3], (N_DOM * N_SUB * HALO_SUB,), 0, V_DEV), jax.random.fold_in(key_of[3], 1), 0, V_DEV - 1).astype(jnp.int32),
        "tile_dst": plant(jax.random.randint(key_of[4], (N_DOM * N_SUB * 2 * SLOTS,), 0, V_DEV // B), jax.random.fold_in(key_of[4], 1), 0, (V_DEV // B) - 1).astype(jnp.int32),
        "inner_src": plant(jax.random.randint(key_of[5], (N_DOM * N_SUB * SLOTS,), 0, V_DEV // B), jax.random.fold_in(key_of[5], 1), 0, (V_DEV // B) - 1).astype(jnp.int32),
        "outer_src": plant(jax.random.randint(key_of[6], (N_DOM * N_SUB * SLOTS,), 0, (HALO_DOM + HALO_SUB) // B), jax.random.fold_in(key_of[6], 1), 0, ((HALO_DOM + HALO_SUB) // B) - 1).astype(jnp.int32),
        "tile_live": plant(jax.random.randint(key_of[7], (N_DOM * N_SUB, 2), SLOTS // 2, SLOTS + 1), jax.random.fold_in(key_of[7], 1), SLOTS // 2, SLOTS).astype(jnp.int32),
        "tile_weight": normal_values(key_of[8], (N_DOM * N_SUB * 2 * SLOTS, B, B), (3 * B) ** -0.5, 0.3125, ((0, 512),)),
    }


epsilon = 1e-05

def whiten_map(gram_sum, vertex_count, feat_width):
    identity = jnp.eye(feat_width, dtype=jnp.float32)
    scaled = gram_sum / vertex_count + epsilon * identity
    lower = jnp.linalg.cholesky(scaled)
    inverse = lax.linalg.triangular_solve(lower, identity, left_side=True, lower=True)
    return inverse.T

def reference(features, weight, send_far, send_near, tile_dst, inner_src, outer_src, tile_live, tile_weight):
    device_total = N_DOM * N_SUB
    local_tiles = V_DEV // B
    blocks = features.reshape(N_DOM, N_SUB, V_DEV, F)
    far_lists = send_far.reshape(N_DOM, N_SUB, N_DOM, PEER_DOM)
    near_lists = send_near.reshape(N_DOM, N_SUB, N_SUB, PEER_SUB)
    dest_tiles = tile_dst.reshape(device_total, 2 * SLOTS)
    inner_tiles = inner_src.reshape(device_total, SLOTS)
    outer_tiles = outer_src.reshape(device_total, SLOTS)
    slot_weights = tile_weight.reshape(device_total, 2 * SLOTS, B, B)

    def per_device(device_index):
        dom_index = device_index // N_SUB
        sub_index = device_index % N_SUB
        same_sub = blocks[:, sub_index]
        far_index = far_lists[:, sub_index, dom_index, :]
        far_rows = jnp.take_along_axis(same_sub, far_index[:, :, None], axis=1).reshape(HALO_DOM, F)
        same_dom = blocks[dom_index]
        near_index = near_lists[dom_index, :, sub_index, :]
        near_rows = jnp.take_along_axis(same_dom, near_index[:, :, None], axis=1).reshape(HALO_SUB, F)
        own_rows = blocks[dom_index, sub_index]
        tile_table = jnp.concatenate([own_rows, far_rows, near_rows], 0).reshape(-1, B, F).astype(jnp.float32)
        source_tiles = jnp.concatenate([inner_tiles[device_index], outer_tiles[device_index] + local_tiles])
        selected = tile_table[source_tiles]
        products = jnp.einsum('kij,kjf->kif', slot_weights[device_index].astype(jnp.float32), selected, precision=lax.Precision.HIGHEST)
        slot_index = jnp.arange(SLOTS, dtype=jnp.int32)
        slot_mask = jnp.concatenate([slot_index < tile_live[device_index, 0], slot_index < tile_live[device_index, 1]])
        tile_index = jnp.arange(local_tiles, dtype=jnp.int32)
        selector = ((dest_tiles[device_index][None, :] == tile_index[:, None]) & slot_mask[None, :]).astype(jnp.float32)
        summed = jnp.einsum('tk,kif->tif', selector, products, precision=lax.Precision.HIGHEST).reshape(V_DEV, F)
        aggregate = summed.astype(jnp.bfloat16)
        projected = jnp.dot(aggregate.astype(jnp.float32), weight.astype(jnp.float32), preferred_element_type=jnp.float32)
        return (own_rows.astype(jnp.float32) + jax.nn.silu(projected)).astype(jnp.bfloat16)
    hidden = lax.map(per_device, jnp.arange(device_total, dtype=jnp.int32)).reshape(VERTS, F)
    gram_sum = lax.dot_general(hidden.astype(jnp.float32), hidden.astype(jnp.float32), (((0,), (0,)), ((), ())), preferred_element_type=jnp.float32)
    whitener = whiten_map(gram_sum, VERTS, F)
    white = jnp.dot(hidden.astype(jnp.float32), whitener, precision=lax.Precision.HIGHEST)
    distance = white - features.astype(jnp.float32)
    loss_value = jnp.sum(distance * distance) / (VERTS * F)
    return (white.astype(jnp.bfloat16), loss_value)
```

```python
import functools

import jax
import jax.numpy as jnp
from jax import lax
from jax.experimental import pallas as pl
from jax.experimental.pallas import tpu as pltpu
from jax.sharding import Mesh
from jax.sharding import PartitionSpec as P

MESH_AXES = ("x", "z", "c", "y")
DOM = ("x", "z", "c")

EPSILON = 1e-05
PANEL = 32
SUB = 8
LANES = 128

VMEM = pl.BlockSpec(memory_space=pltpu.VMEM)
SMEM = pl.BlockSpec(memory_space=pltpu.SMEM)


def iota(shape, dim):
    return lax.broadcasted_iota(jnp.int32, shape, dim)


def contract(a, b, dims, **kw):
    return lax.dot_general(a, b, (dims, ((), ())), preferred_element_type=jnp.float32, **kw)


def three_terms(x):
    high = x.astype(jnp.bfloat16)
    rest = x - high.astype(jnp.float32)
    middle = rest.astype(jnp.bfloat16)
    low = (rest - middle.astype(jnp.float32)).astype(jnp.bfloat16)
    return high, middle, low


def reciprocal_of(p):
    guess = pl.reciprocal(p, approx=True)
    guess = guess * (2.0 - p * guess)
    return guess * (2.0 - p * guess)


def eliminate_panel(rows, near, first_lane, width):
    groups = PANEL // SUB
    rows, near = list(rows), list(near)
    lane = iota((SUB, width), 1)
    sub = iota((SUB, width), 0)
    sub_lane = iota((SUB, LANES), 0)
    pivots = [None] * groups
    full = (SUB, LANES)
    for b in range(groups):
        start = first_lane + SUB * b
        in_block = (lane >= start) & (lane < start + SUB)
        unit = jnp.where(lane - start == sub, 1.0, 0.0)
        rows[b] = jnp.where(in_block, unit, rows[b])
        for g in range(b + 1, groups):
            rows[g] = jnp.where(in_block, 0.0, rows[g])
        column = [
            {g: jnp.broadcast_to(near[g][:, SUB * b + k : SUB * b + k + 1], full) for g in range(b, groups)}
            for k in range(SUB)
        ]
        entry = {
            (m, k): jnp.broadcast_to(column[k][b][m : m + 1, :], full) for k in range(SUB) for m in range(k, SUB)
        }
        pivot = jnp.ones(full, jnp.float32)
        for k in range(SUB):
            inverse = reciprocal_of(entry[k, k])
            pivot = jnp.where(sub_lane == k, entry[k, k], pivot)
            ratio = {m: entry[m, k] * inverse for m in range(k + 1, SUB)}
            for n in range(k + 1, SUB):
                for m in range(n, SUB):
                    entry[m, n] = entry[m, n] - ratio[m] * entry[n, k]
            scale = {g: column[k][g] * inverse for g in range(b, groups)}
            scale[b] = jnp.where(sub_lane > k, scale[b], 0.0)
            for m in range(k + 1, SUB):
                for g in range(b, groups):
                    column[m][g] = column[m][g] - scale[g] * entry[m, k]
            lead = jnp.broadcast_to(rows[b][k : k + 1, :], (SUB, width))
            lead_near = jnp.broadcast_to(near[b][k : k + 1, :], full)
            for g in range(b, groups):
                wide = jnp.concatenate([scale[g]] * (width // LANES), 1)
                rows[g] = rows[g] - wide * lead
            near[b] = near[b] - scale[b] * lead_near
            for g in range(b + 1, groups):
                near[g] = near[g] - scale[g] * lead_near
        pivots[b] = pivot
    return rows, pivots


def whiten_kernel(vertex_count, parts_ref, hidden_ref, white_ref, loss_ref, a_ref, v_ref):
    width = a_ref.shape[0]
    groups = PANEL // SUB
    left = parts_ref[:, 0:SUB, :].reshape(width, LANES)
    right = parts_ref[:, SUB : 2 * SUB, :].reshape(width, LANES)
    packed = jnp.concatenate([left, right], 1)
    row, col = iota((width, width), 0), iota((width, width), 1)
    gram = jnp.where(row >= col, packed, packed.T)
    a_ref[...] = gram / vertex_count + jnp.where(row == col, EPSILON, 0.0)

    def panel(j, carry):
        first = pl.multiple_of(j * PANEL, PANEL)
        block = a_ref[pl.ds(first, PANEL), :]
        turned = pltpu.roll(block, lax.rem(width - first, width), 1)[:, :LANES]
        rows, pivots = eliminate_panel(
            [block[SUB * g : SUB * g + SUB] for g in range(groups)],
            [turned[SUB * g : SUB * g + SUB] for g in range(groups)],
            first,
            width,
        )
        whole = jnp.concatenate(rows, 0)
        pivot = jnp.concatenate(pivots, 0)
        pivot = jnp.concatenate([pivot] * (width // LANES), 1)
        lane = iota((PANEL, width), 1)
        lower = lane <= iota((PANEL, width), 0) + first
        v_ref[pl.ds(first, PANEL), :] = jnp.where(lower, whole * lax.rsqrt(pivot), 0.0)
        h, m, l = three_terms(whole / pivot)
        hh, mm, ll = three_terms(jnp.where(lower | (lane >= first + PANEL), whole, 0.0))
        update = contract(
            jnp.concatenate([h, h, m, h, l, m], 0), jnp.concatenate([hh, mm, hh, ll, hh, mm], 0), ((0,), (0,))
        )
        lanes = iota((width, width), 1)
        kept = jnp.where((lanes >= first) & (lanes < first + PANEL), 0.0, a_ref[...])
        a_ref[...] = kept - update
        return carry

    lax.fori_loop(0, width // PANEL, panel, 0)

    inverse = v_ref[...]
    high = inverse.astype(jnp.bfloat16)
    low = (inverse - high.astype(jnp.float32)).astype(jnp.bfloat16)
    hidden = hidden_ref[...]
    white_ref[...] = (contract(hidden, high, ((1,), (1,))) + contract(hidden, low, ((1,), (1,)))).astype(white_ref.dtype)

    left = parts_ref[:, 0:SUB, :].reshape(width, LANES)
    right = parts_ref[:, SUB : 2 * SUB, :].reshape(width, LANES)
    packed = jnp.concatenate([left, right], 1)
    turned = packed.T
    gram = jnp.where(row >= col, packed, turned)
    cross = jnp.where(row > col, turned, 0.0)
    spare = parts_ref[:, 2 * SUB : 3 * SUB, :].reshape(width, LANES)
    square_sum = spare[0, LANES - 1]
    image = contract(inverse, gram, ((1,), (0,)), precision=lax.Precision.HIGHEST)
    half = row[:, :LANES] < LANES
    diagonal = jnp.where(half, inverse[:, :LANES], inverse[:, LANES:]) * spare
    doubled = inverse * (image - 2.0 * cross)
    total = jnp.sum(doubled) - 2.0 * jnp.sum(diagonal) + square_sum
    loss_ref[0, 0] = total / (vertex_count * width)


def whiten(parts, hidden, vertex_count):
    rows, width = hidden.shape
    return pl.pallas_call(
        functools.partial(whiten_kernel, vertex_count),
        out_shape=(jax.ShapeDtypeStruct((rows, width), jnp.bfloat16), jax.ShapeDtypeStruct((1, 1), jnp.float32)),
        in_specs=[VMEM, VMEM],
        out_specs=(VMEM, SMEM),
        scratch_shapes=[pltpu.VMEM((width, width), jnp.float32), pltpu.VMEM((width, width), jnp.float32)],
        compiler_params=pltpu.CompilerParams(vmem_limit_bytes=24 * 2**20),
    )(parts, hidden)


def pack(gram, cross, square_sum):
    width = gram.shape[0]
    row, col = iota((width, width), 0), iota((width, width), 1)
    both = jnp.where(row >= col, gram, cross)
    diagonal = jnp.where(row == col, cross, 0.0)
    half = row[:, :LANES] < LANES
    spare = jnp.where(half, diagonal[:, :LANES], diagonal[:, LANES:])
    corner = (row[:, :LANES] == 0) & (col[:, :LANES] == LANES - 1)
    spare = jnp.where(corner, square_sum, spare)
    shape = (width // SUB, SUB, LANES)
    return [both[:, :LANES].reshape(shape), both[:, LANES:].reshape(shape), spare.reshape(shape)]


def gather_kernel(features_ref, index_ref, out_ref):
    source = features_ref.shape[0]
    chunks = index_ref.shape[0]
    lane = iota((LANES, LANES), 1)
    features = features_ref[...]
    for r in range(chunks):
        wanted = jnp.broadcast_to(index_ref[r : r + 1, :].astype(jnp.float32), (LANES, LANES)).T.astype(jnp.int32)
        picks = [
            jnp.where(wanted == lane + LANES * s, 1.0, 0.0).astype(jnp.bfloat16) for s in range(source // LANES)
        ]
        picked = contract(jnp.concatenate(picks, 1), features, ((1,), (0,)))
        out_ref[LANES * r : LANES * r + LANES, :] = picked.astype(out_ref.dtype)


def gather(features, index):
    return pl.pallas_call(
        gather_kernel,
        out_shape=jax.ShapeDtypeStruct((index.size, features.shape[1]), features.dtype),
        in_specs=[VMEM, VMEM],
        out_specs=VMEM,
        compiler_params=pltpu.CompilerParams(vmem_limit_bytes=24 * 2**20),
    )(features, index.reshape(-1, LANES))


def layer_kernel(
    dst_ref, inner_ref, outer_ref, live_ref, features_ref, far_ref, near_ref, tile_ref, weight_ref,
    hidden_ref, parts_ref, sum_ref,
):
    slots, tile = inner_ref.shape[0], tile_ref.shape[1]
    far_tiles = far_ref.shape[0] // tile
    sum_ref[...] = jnp.zeros_like(sum_ref)

    def add(c, source):
        to = pl.ds(pl.multiple_of(dst_ref[c] * tile, tile), tile)
        sum_ref[to, :] += contract(tile_ref[c], source, ((1,), (0,)))

    def rows_of(ref, index):
        return ref[pl.ds(pl.multiple_of(index * tile, tile), tile), :]

    for k in range(slots):
        @pl.when(k < live_ref[0, 0])
        def _(k=k):
            add(k, rows_of(features_ref, inner_ref[k]))

        @pl.when((k < live_ref[0, 1]) & (outer_ref[k] < far_tiles))
        def _(k=k):
            add(slots + k, rows_of(far_ref, outer_ref[k]))

        @pl.when((k < live_ref[0, 1]) & (outer_ref[k] >= far_tiles))
        def _(k=k):
            add(slots + k, rows_of(near_ref, outer_ref[k] - far_tiles))

    projected = contract(sum_ref[...].astype(jnp.bfloat16), weight_ref[...], ((1,), (0,)))
    features = features_ref[...]
    wide = features.astype(jnp.float32)
    hidden = (wide + projected / (1.0 + jnp.exp(-projected))).astype(jnp.bfloat16)
    hidden_ref[...] = hidden
    gram = contract(hidden, hidden, ((0,), (0,)))
    cross = contract(hidden, features, ((0,), (0,)))
    for i, part in enumerate(pack(gram, cross, jnp.sum(wide * wide))):
        parts_ref[:, SUB * i : SUB * i + SUB, :] = part


def layer(dst, inner, outer, live, features, far, near, tiles, weight):
    rows, width = features.shape
    return pl.pallas_call(
        layer_kernel,
        out_shape=(
            jax.ShapeDtypeStruct((rows, width), jnp.bfloat16),
            jax.ShapeDtypeStruct((width // SUB, 3 * SUB, LANES), jnp.float32),
        ),
        in_specs=[SMEM] * 4 + [VMEM] * 5,
        out_specs=(VMEM, VMEM),
        scratch_shapes=[pltpu.VMEM((rows, width), jnp.float32)],
        compiler_params=pltpu.CompilerParams(vmem_limit_bytes=32 * 2**20),
    )(dst, inner, outer, live, features, far, near, tiles, weight)


def sum_over_all(parts):
    own = jnp.sum(lax.all_to_all(parts, ("x", "c", "y"), 0, 0, tiled=True), 0)
    z_size = lax.axis_size("z")
    own = jnp.broadcast_to(own[None], (z_size, *own.shape))
    own = jnp.sum(lax.all_to_all(own, "z", 0, 0, tiled=True), 0)
    own = jnp.broadcast_to(own[None], parts.shape)
    return lax.all_to_all(own, ("x", "c", "y"), 0, 0, tiled=True)


def body(
    features, weight, send_far, send_near, tile_dst, inner_src, outer_src, tile_live, tile_weight
):
    rows = features.shape[0]
    picked = gather(features, jnp.concatenate([send_far, send_near]))
    far_count = send_far.shape[0]
    far = picked[:far_count].reshape(lax.axis_size(DOM), -1, features.shape[1])
    far = lax.all_to_all(far, DOM, 0, 0, tiled=True).reshape(far_count, -1)
    near = lax.all_to_all(picked[far_count:], "y", 0, 0, tiled=True)
    hidden, parts = layer(
        tile_dst, inner_src, outer_src, tile_live, features, far, near, tile_weight, weight
    )
    parts = sum_over_all(parts)
    vertex_count = rows * lax.axis_size(DOM) * lax.axis_size("y")
    white, loss = whiten(parts, hidden, vertex_count)
    return white, loss[0, 0]


def solution(mesh):
    torus = Mesh(mesh.devices.reshape(4, 16, 2, mesh.shape["sub"]), MESH_AXES)
    whole = MESH_AXES
    return jax.shard_map(
        body,
        mesh=torus,
        in_specs=(
            P(whole, None), P(), P(whole), P(whole), P(whole), P(whole), P(whole), P(whole, None), P(whole, None, None),
        ),
        out_specs=(P(whole, None), P()),
        check_vma=False,
    )
```

```python
import functools

import jax
import jax.numpy as jnp
from jax import lax
from jax.experimental import pallas as pl
from jax.experimental.pallas import tpu as pltpu
from jax.sharding import Mesh
from jax.sharding import PartitionSpec as P

MESH_AXES = ("x", "z", "c", "y")
DOM = ("x", "z", "c")

EPSILON = 1e-05
PANEL = 32
SUB = 8
LANES = 128

VMEM = pl.BlockSpec(memory_space=pltpu.VMEM)
SMEM = pl.BlockSpec(memory_space=pltpu.SMEM)


def iota(shape, dim):
    return lax.broadcasted_iota(jnp.int32, shape, dim)


def contract(a, b, dims, **kw):
    return lax.dot_general(a, b, (dims, ((), ())), preferred_element_type=jnp.float32, **kw)


def three_terms(x):
    high = x.astype(jnp.bfloat16)
    rest = x - high.astype(jnp.float32)
    middle = rest.astype(jnp.bfloat16)
    low = (rest - middle.astype(jnp.float32)).astype(jnp.bfloat16)
    return high, middle, low


def reciprocal_of(p):
    guess = pl.reciprocal(p, approx=True)
    guess = guess * (2.0 - p * guess)
    return guess * (2.0 - p * guess)


def eliminate_panel(rows, near, first_lane, width):
    groups = PANEL // SUB
    rows, near = list(rows), list(near)
    lane = iota((SUB, width), 1)
    sub = iota((SUB, width), 0)
    sub_lane = iota((SUB, LANES), 0)
    pivots = [None] * groups
    full = (SUB, LANES)
    for b in range(groups):
        start = first_lane + SUB * b
        in_block = (lane >= start) & (lane < start + SUB)
        unit = jnp.where(lane - start == sub, 1.0, 0.0)
        rows[b] = jnp.where(in_block, unit, rows[b])
        for g in range(b + 1, groups):
            rows[g] = jnp.where(in_block, 0.0, rows[g])
        column = [
            {g: jnp.broadcast_to(near[g][:, SUB * b + k : SUB * b + k + 1], full) for g in range(b, groups)}
            for k in range(SUB)
        ]
        entry = {
            (m, k): jnp.broadcast_to(column[k][b][m : m + 1, :], full) for k in range(SUB) for m in range(k, SUB)
        }
        pivot = jnp.ones(full, jnp.float32)
        for k in range(SUB):
            inverse = reciprocal_of(entry[k, k])
            pivot = jnp.where(sub_lane == k, entry[k, k], pivot)
            ratio = {m: entry[m, k] * inverse for m in range(k + 1, SUB)}
            for n in range(k + 1, SUB):
                for m in range(n, SUB):
                    entry[m, n] = entry[m, n] - ratio[m] * entry[n, k]
            scale = {g: column[k][g] * inverse for g in range(b, groups)}
            scale[b] = jnp.where(sub_lane > k, scale[b], 0.0)
            for m in range(k + 1, SUB):
                for g in range(b, groups):
                    column[m][g] = column[m][g] - scale[g] * entry[m, k]
            lead = jnp.broadcast_to(rows[b][k : k + 1, :], (SUB, width))
            lead_near = jnp.broadcast_to(near[b][k : k + 1, :], full)
            for g in range(b, groups):
                wide = jnp.concatenate([scale[g]] * (width // LANES), 1)
                rows[g] = rows[g] - wide * lead
            near[b] = near[b] - scale[b] * lead_near
            for g in range(b + 1, groups):
                near[g] = near[g] - scale[g] * lead_near
        pivots[b] = pivot
    return rows, pivots


def whiten_kernel(vertex_count, parts_ref, hidden_ref, white_ref, loss_ref, a_ref, v_ref):
    width = a_ref.shape[0]
    groups = PANEL // SUB
    left = parts_ref[:, 0:SUB, :].reshape(width, LANES)
    right = parts_ref[:, SUB : 2 * SUB, :].reshape(width, LANES)
    packed = jnp.concatenate([left, right], 1)
    row, col = iota((width, width), 0), iota((width, width), 1)
    gram = jnp.where(row >= col, packed, packed.T)
    a_ref[...] = gram / vertex_count + jnp.where(row == col, EPSILON, 0.0)

    def panel(j, carry):
        first = pl.multiple_of(j * PANEL, PANEL)
        block = a_ref[pl.ds(first, PANEL), :]
        turned = pltpu.roll(block, lax.rem(width - first, width), 1)[:, :LANES]
        rows, pivots = eliminate_panel(
            [block[SUB * g : SUB * g + SUB] for g in range(groups)],
            [turned[SUB * g : SUB * g + SUB] for g in range(groups)],
            first,
            width,
        )
        whole = jnp.concatenate(rows, 0)
        pivot = jnp.concatenate(pivots, 0)
        pivot = jnp.concatenate([pivot] * (width // LANES), 1)
        lane = iota((PANEL, width), 1)
        lower = lane <= iota((PANEL, width), 0) + first
        v_ref[pl.ds(first, PANEL), :] = jnp.where(lower, whole * lax.rsqrt(pivot), 0.0)
        h, m, l = three_terms(whole / pivot)
        hh, mm, ll = three_terms(jnp.where(lower | (lane >= first + PANEL), whole, 0.0))
        update = contract(
            jnp.concatenate([h, h, m, h, l, m], 0), jnp.concatenate([hh, mm, hh, ll, hh, mm], 0), ((0,), (0,))
        )
        lanes = iota((width, width), 1)
        kept = jnp.where((lanes >= first) & (lanes < first + PANEL), 0.0, a_ref[...])
        a_ref[...] = kept - update
        return carry

    lax.fori_loop(0, width // PANEL, panel, 0)

    inverse = v_ref[...]
    high = inverse.astype(jnp.bfloat16)
    low = (inverse - high.astype(jnp.float32)).astype(jnp.bfloat16)
    hidden = hidden_ref[...]
    white_ref[...] = (contract(hidden, high, ((1,), (1,))) + contract(hidden, low, ((1,), (1,)))).astype(white_ref.dtype)

    left = parts_ref[:, 0:SUB, :].reshape(width, LANES)
    right = parts_ref[:, SUB : 2 * SUB, :].reshape(width, LANES)
    packed = jnp.concatenate([left, right], 1)
    turned = packed.T
    gram = jnp.where(row >= col, packed, turned)
    cross = jnp.where(row > col, turned, 0.0)
    spare = parts_ref[:, 2 * SUB : 3 * SUB, :].reshape(width, LANES)
    square_sum = spare[0, LANES - 1]
    image = contract(inverse, gram, ((1,), (0,)), precision=lax.Precision.HIGHEST)
    half = row[:, :LANES] < LANES
    diagonal = jnp.where(half, inverse[:, :LANES], inverse[:, LANES:]) * spare
    doubled = inverse * (image - 2.0 * cross)
    total = jnp.sum(doubled) - 2.0 * jnp.sum(diagonal) + square_sum
    loss_ref[0, 0] = total / (vertex_count * width)


def whiten(parts, hidden, vertex_count):
    rows, width = hidden.shape
    return pl.pallas_call(
        functools.partial(whiten_kernel, vertex_count),
        out_shape=(jax.ShapeDtypeStruct((rows, width), jnp.bfloat16), jax.ShapeDtypeStruct((1, 1), jnp.float32)),
        in_specs=[VMEM, VMEM],
        out_specs=(VMEM, SMEM),
        scratch_shapes=[pltpu.VMEM((width, width), jnp.float32), pltpu.VMEM((width, width), jnp.float32)],
        compiler_params=pltpu.CompilerParams(vmem_limit_bytes=24 * 2**20),
    )(parts, hidden)


def pack(gram, cross, square_sum):
    width = gram.shape[0]
    row, col = iota((width, width), 0), iota((width, width), 1)
    both = jnp.where(row >= col, gram, cross)
    diagonal = jnp.where(row == col, cross, 0.0)
    half = row[:, :LANES] < LANES
    spare = jnp.where(half, diagonal[:, :LANES], diagonal[:, LANES:])
    corner = (row[:, :LANES] == 0) & (col[:, :LANES] == LANES - 1)
    spare = jnp.where(corner, square_sum, spare)
    shape = (width // SUB, SUB, LANES)
    return [both[:, :LANES].reshape(shape), both[:, LANES:].reshape(shape), spare.reshape(shape)]


def gather_kernel(place_ref, features_ref, far_index_ref, near_index_ref, far_ref, turned_ref, near_own_ref, *near_refs):
    source, width = features_ref.shape
    lane = iota((LANES, LANES), 1)
    features = features_ref[...]

    def rows_at(index):
        wanted = jnp.broadcast_to(index.astype(jnp.float32), (LANES, LANES)).T.astype(jnp.int32)
        picks = [
            jnp.where(wanted == lane + LANES * s, 1.0, 0.0).astype(jnp.bfloat16) for s in range(source // LANES)
        ]
        return contract(jnp.concatenate(picks, 1), features, ((1,), (0,)))

    for r in range(far_index_ref.shape[0]):
        picked = rows_at(far_index_ref[r : r + 1, :])
        here = slice(LANES * r, LANES * r + LANES)
        far_ref[here, :] = picked.astype(far_ref.dtype)
        turned = pltpu.roll(picked.reshape(LANES // SUB, SUB, width), SUB // 2, 1)
        turned_ref[here, :] = turned.reshape(LANES, width).astype(turned_ref.dtype)
    picked = rows_at(near_index_ref[...]).astype(near_own_ref.dtype)
    peers = 1 + len(near_refs)
    block = LANES // peers
    for k, ref in enumerate((near_own_ref, *near_refs)):
        for q in range(peers):
            @pl.when(lax.rem(place_ref[1] + k, peers) == q)
            def _(ref=ref, q=q):
                ref[...] = picked[block * q : block * q + block]


def gather(place, features, far_index, near_index, peers):
    width, dtype = features.shape[1], features.dtype
    far = jax.ShapeDtypeStruct((far_index.size, width), dtype)
    near = jax.ShapeDtypeStruct((near_index.size // peers, width), dtype)
    return pl.pallas_call(
        gather_kernel,
        out_shape=(far, far) + (near,) * peers,
        in_specs=[SMEM, VMEM, VMEM, VMEM],
        out_specs=(VMEM,) * (2 + peers),
        compiler_params=pltpu.CompilerParams(vmem_limit_bytes=24 * 2**20),
    )(place, features, far_index.reshape(-1, LANES), near_index.reshape(-1, LANES))


def layer_kernel(
    place_ref, dst_ref, inner_ref, outer_ref, live_ref, features_ref, far_ref, tile_ref, weight_ref, *rest
):
    *near_refs, hidden_ref, parts_ref, sum_ref, near_ref = rest
    peers = len(near_refs)
    block = near_ref.shape[0] // peers
    for k, ref in enumerate(near_refs):
        at = lax.rem(place_ref[1] + peers - k, peers)
        near_ref[pl.ds(pl.multiple_of(at * block, block), block), :] = ref[...]
    slots, tile = inner_ref.shape[0], tile_ref.shape[1]
    far_tiles = far_ref.shape[0] // tile
    sum_ref[...] = jnp.zeros_like(sum_ref)

    def add(c, source):
        to = pl.ds(pl.multiple_of(dst_ref[c] * tile, tile), tile)
        sum_ref[to, :] += contract(tile_ref[c], source, ((1,), (0,)))

    def rows_of(ref, index):
        return ref[pl.ds(pl.multiple_of(index * tile, tile), tile), :]

    for k in range(slots):
        @pl.when(k < live_ref[0, 0])
        def _(k=k):
            add(k, rows_of(features_ref, inner_ref[k]))

        @pl.when((k < live_ref[0, 1]) & (outer_ref[k] < far_tiles))
        def _(k=k):
            add(slots + k, rows_of(far_ref, outer_ref[k]))

        @pl.when((k < live_ref[0, 1]) & (outer_ref[k] >= far_tiles))
        def _(k=k):
            add(slots + k, rows_of(near_ref, outer_ref[k] - far_tiles))

    projected = contract(sum_ref[...].astype(jnp.bfloat16), weight_ref[...], ((1,), (0,)))
    features = features_ref[...]
    wide = features.astype(jnp.float32)
    hidden = (wide + projected / (1.0 + jnp.exp(-projected))).astype(jnp.bfloat16)
    hidden_ref[...] = hidden
    gram = contract(hidden, hidden, ((0,), (0,)))
    cross = contract(hidden, features, ((0,), (0,)))
    for i, part in enumerate(pack(gram, cross, jnp.sum(wide * wide))):
        parts_ref[:, SUB * i : SUB * i + SUB, :] = part


def layer(place, dst, inner, outer, live, features, far, tiles, weight, near):
    rows, width = features.shape
    near_rows = sum(n.shape[0] for n in near)
    return pl.pallas_call(
        layer_kernel,
        out_shape=(
            jax.ShapeDtypeStruct((rows, width), jnp.bfloat16),
            jax.ShapeDtypeStruct((width // SUB, 3 * SUB, LANES), jnp.float32),
        ),
        in_specs=[SMEM] * 5 + [VMEM] * (4 + len(near)),
        out_specs=(VMEM, VMEM),
        scratch_shapes=[pltpu.VMEM((rows, width), jnp.float32), pltpu.VMEM((near_rows, width), features.dtype)],
        compiler_params=pltpu.CompilerParams(vmem_limit_bytes=32 * 2**20),
    )(place, dst, inner, outer, live, features, far, tiles, weight, *near)


def sum_over_all(parts):
    own = jnp.sum(lax.all_to_all(parts, ("x", "c", "y"), 0, 0, tiled=True), 0)
    z_size = lax.axis_size("z")
    own = jnp.broadcast_to(own[None], (z_size, *own.shape))
    own = jnp.sum(lax.all_to_all(own, "z", 0, 0, tiled=True), 0)
    own = jnp.broadcast_to(own[None], parts.shape)
    return lax.all_to_all(own, ("x", "c", "y"), 0, 0, tiled=True)


def body(
    features, weight, send_far, send_near, tile_dst, inner_src, outer_src, tile_live, tile_weight
):
    rows, width = features.shape
    core, y = lax.axis_index("c"), lax.axis_index("y")
    peers = lax.axis_size("y")
    place = jnp.stack([core, y]).astype(jnp.int32)
    far, turned, *near = gather(place, features, send_far, send_near, peers)
    crossed = lax.ppermute(turned, "c", [(0, 1), (1, 0)])
    upper = iota((1, SUB, 1), 1) >= SUB // 2
    mixed = jnp.where(upper == (core == 1), far.reshape(-1, SUB, width), crossed.reshape(-1, SUB, width))
    far = lax.all_to_all(mixed, ("x", "z"), 0, 0, tiled=True).reshape(-1, width)
    near = near[:1] + [
        lax.ppermute(near[k], "y", [(i, (i + k) % peers) for i in range(peers)]) for k in range(1, peers)
    ]
    hidden, parts = layer(
        place, tile_dst, inner_src, outer_src, tile_live, features, far, tile_weight, weight, near
    )
    parts = sum_over_all(parts)
    vertex_count = rows * lax.axis_size(DOM) * lax.axis_size("y")
    white, loss = whiten(parts, hidden, vertex_count)
    return white, loss[0, 0]


def solution(mesh):
    torus = Mesh(mesh.devices.reshape(4, 16, 2, mesh.shape["sub"]), MESH_AXES)
    whole = MESH_AXES
    return jax.shard_map(
        body,
        mesh=torus,
        in_specs=(
            P(whole, None), P(), P(whole), P(whole), P(whole), P(whole), P(whole), P(whole, None), P(whole, None, None),
        ),
        out_specs=(P(whole, None), P()),
        check_vma=False,
    )
```

```python
import functools

import jax
import jax.numpy as jnp
from jax import lax
from jax.experimental import pallas as pl
from jax.experimental.pallas import tpu as pltpu
from jax.sharding import Mesh
from jax.sharding import PartitionSpec as P

MESH_AXES = ("x", "z", "c", "y")
DOM = ("x", "z", "c")

EPSILON = 1e-05
PANEL = 32
SUB = 8
LANES = 128

VMEM = pl.BlockSpec(memory_space=pltpu.VMEM)
SMEM = pl.BlockSpec(memory_space=pltpu.SMEM)


def iota(shape, dim):
    return lax.broadcasted_iota(jnp.int32, shape, dim)


def contract(a, b, dims, **kw):
    return lax.dot_general(a, b, (dims, ((), ())), preferred_element_type=jnp.float32, **kw)


def three_terms(x):
    high = x.astype(jnp.bfloat16)
    rest = x - high.astype(jnp.float32)
    middle = rest.astype(jnp.bfloat16)
    low = (rest - middle.astype(jnp.float32)).astype(jnp.bfloat16)
    return high, middle, low


def eliminate_panel(rows, near, first_lane, width):
    groups = PANEL // SUB
    rows, near = list(rows), list(near)
    lane = iota((SUB, width), 1)
    sub = iota((SUB, width), 0)
    sub_lane = iota((SUB, LANES), 0)
    pivots = [None] * groups
    full = (SUB, LANES)
    for b in range(groups):
        start = first_lane + SUB * b
        in_block = (lane >= start) & (lane < start + SUB)
        unit = jnp.where(lane - start == sub, 1.0, 0.0)
        rows[b] = jnp.where(in_block, unit, rows[b])
        for g in range(b + 1, groups):
            rows[g] = jnp.where(in_block, 0.0, rows[g])
        column = [
            {g: jnp.take_along_axis(near[g], jnp.full(full, SUB * b + k, jnp.int32), 1, mode='promise_in_bounds') for g in range(b, groups)}
            for k in range(SUB)
        ]
        entry = {
            (m, k): jnp.broadcast_to(column[k][b][m : m + 1, :], full) for k in range(SUB) for m in range(k, SUB)
        }
        pivot = jnp.ones(full, jnp.float32)
        for k in range(0, SUB, 2):
            p, side, q = entry[k, k], entry[k + 1, k], entry[k + 1, k + 1]
            det = p * q - side * side
            inverse = pl.reciprocal(p)
            both = pl.reciprocal(p * det)
            second = both * p
            pivot = jnp.where(sub_lane == k, p, jnp.where(sub_lane == k + 1, det * inverse, pivot))
            left = {m: entry[m, k] for m in range(k + 2, SUB)}
            right = {m: p * entry[m, k + 1] - side * entry[m, k] for m in range(k + 2, SUB)}
            for n in range(k + 2, SUB):
                for m in range(n, SUB):
                    entry[m, n] = (entry[m, n] - left[m] * left[n] * inverse) - right[m] * right[n] * both
            first_scale, second_scale = {}, {}
            for g in range(b, groups):
                x, y = column[k][g], column[k + 1][g]
                first_scale[g] = x * inverse
                second_scale[g] = (p * y - side * x) * second
            first_scale[b] = jnp.where(sub_lane > k, first_scale[b], 0.0)
            second_scale[b] = jnp.where(sub_lane > k + 1, second_scale[b], 0.0)
            for m in range(k + 2, SUB):
                reduced = right[m] * inverse
                for g in range(b, groups):
                    column[m][g] = column[m][g] - first_scale[g] * left[m] - second_scale[g] * reduced
            ratio = side * inverse

            def lead_of(x):
                shape = (SUB, x.shape[1])
                first = jnp.broadcast_to(x[k : k + 1, :], shape)
                wide = jnp.concatenate([ratio] * (x.shape[1] // LANES), 1)
                return first, jnp.broadcast_to(x[k + 1 : k + 2, :], shape) - wide * first

            lead = lead_of(rows[b])
            lead_near = lead_of(near[b])
            for g in range(b, groups):
                one = jnp.concatenate([first_scale[g]] * (width // LANES), 1)
                two = jnp.concatenate([second_scale[g]] * (width // LANES), 1)
                rows[g] = rows[g] - one * lead[0] - two * lead[1]
                near[g] = near[g] - first_scale[g] * lead_near[0] - second_scale[g] * lead_near[1]
        pivots[b] = pivot
    return rows, pivots


def whiten_kernel(vertex_count, parts_ref, hidden_ref, white_ref, loss_ref, a_ref, v_ref):
    width = a_ref.shape[0]
    groups = PANEL // SUB
    packed = jnp.concatenate([parts_ref[:width, :], parts_ref[width : 2 * width, :]], 1)
    row, col = iota((width, width), 0), iota((width, width), 1)
    gram = jnp.where(row >= col, packed, packed.T)
    a_ref[...] = gram / vertex_count + jnp.where(row == col, EPSILON, 0.0)

    def panel(j, carry):
        first = pl.multiple_of(j * PANEL, PANEL)
        block = a_ref[pl.ds(first, PANEL), :]
        turned = pltpu.roll(block, lax.rem(width - first, width), 1)[:, :LANES]
        rows, pivots = eliminate_panel(
            [block[SUB * g : SUB * g + SUB] for g in range(groups)],
            [turned[SUB * g : SUB * g + SUB] for g in range(groups)],
            first,
            width,
        )
        whole = jnp.concatenate(rows, 0)
        pivot = jnp.concatenate(pivots, 0)
        pivot = jnp.concatenate([pivot] * (width // LANES), 1)
        lane = iota((PANEL, width), 1)
        lower = lane <= iota((PANEL, width), 0) + first
        v_ref[pl.ds(first, PANEL), :] = jnp.where(lower, whole * lax.rsqrt(pivot), 0.0)
        h, m, l = three_terms(whole / pivot)
        hh, mm, ll = three_terms(jnp.where(lower | (lane >= first + PANEL), whole, 0.0))
        update = contract(
            jnp.concatenate([h, h, m, h, l, m], 0), jnp.concatenate([hh, mm, hh, ll, hh, mm], 0), ((0,), (0,))
        )
        lanes = iota((width, width), 1)
        kept = jnp.where((lanes >= first) & (lanes < first + PANEL), 0.0, a_ref[...])
        a_ref[...] = kept - update
        return carry

    lax.fori_loop(0, width // PANEL, panel, 0, unroll=True)

    inverse = v_ref[...]
    high = inverse.astype(jnp.bfloat16)
    low = (inverse - high.astype(jnp.float32)).astype(jnp.bfloat16)
    hidden = hidden_ref[...]
    white_ref[...] = (contract(hidden, high, ((1,), (1,))) + contract(hidden, low, ((1,), (1,)))).astype(white_ref.dtype)

    packed = jnp.concatenate([parts_ref[:width, :], parts_ref[width : 2 * width, :]], 1)
    turned = packed.T
    gram = jnp.where(row >= col, packed, turned)
    cross = jnp.where(row > col, turned, 0.0)
    spare = parts_ref[2 * width :, :]
    square_sum = spare[0, LANES - 1]
    image = contract(inverse, gram, ((1,), (0,)), precision=lax.Precision.HIGHEST)
    diagonal = diagonal_of(inverse) * spare
    doubled = inverse * (image - 2.0 * cross)
    total = jnp.sum(doubled) - 2.0 * jnp.sum(diagonal) + square_sum
    loss_ref[0, 0] = total / (vertex_count * width)


def whiten(parts, hidden, vertex_count):
    rows, width = hidden.shape
    return pl.pallas_call(
        functools.partial(whiten_kernel, vertex_count),
        out_shape=(jax.ShapeDtypeStruct((rows, width), jnp.bfloat16), jax.ShapeDtypeStruct((1, 1), jnp.float32)),
        in_specs=[VMEM, VMEM],
        out_specs=(VMEM, SMEM),
        scratch_shapes=[pltpu.VMEM((width, width), jnp.float32), pltpu.VMEM((width, width), jnp.float32)],
        compiler_params=pltpu.CompilerParams(vmem_limit_bytes=24 * 2**20),
    )(parts, hidden)


def diagonal_of(square):
    width = square.shape[0]
    row, col = iota((width, width), 0), iota((width, width), 1)
    kept = jnp.where(row == col, square, 0.0)
    kept = jnp.where(row[:, :LANES] < LANES, kept[:, :LANES], kept[:, LANES:])
    return jnp.sum(kept.reshape(width // SUB, SUB, LANES), 1)


def pack(gram, cross, square_sum):
    width = gram.shape[0]
    row, col = iota((width, width), 0), iota((width, width), 1)
    both = jnp.where(row >= col, gram, cross)
    spare = diagonal_of(cross)
    corner = (iota(spare.shape, 0) == 0) & (iota(spare.shape, 1) == LANES - 1)
    return [both[:, :LANES], both[:, LANES:], jnp.where(corner, square_sum, spare)]


def gather_kernel(place_ref, features_ref, far_index_ref, near_index_ref, far_ref, turned_ref, near_own_ref, *near_refs):
    source, width = features_ref.shape
    lane = iota((LANES, LANES), 1)
    features = features_ref[...]

    def rows_at(index):
        wanted = jnp.broadcast_to(index.astype(jnp.float32), (LANES, LANES)).T.astype(jnp.int32)
        picks = [
            jnp.where(wanted == lane + LANES * s, 1.0, 0.0).astype(jnp.bfloat16) for s in range(source // LANES)
        ]
        return contract(jnp.concatenate(picks, 1), features, ((1,), (0,)))

    for r in range(far_index_ref.shape[0]):
        picked = rows_at(far_index_ref[r : r + 1, :])
        here = slice(LANES * r, LANES * r + LANES)
        far_ref[here, :] = picked.astype(far_ref.dtype)
        turned = pltpu.roll(picked.reshape(LANES // SUB, SUB, width), SUB // 2, 1)
        turned_ref[here, :] = turned.reshape(LANES, width).astype(turned_ref.dtype)
    picked = rows_at(near_index_ref[...]).astype(near_own_ref.dtype)
    peers = 1 + len(near_refs)
    block = LANES // peers
    for k, ref in enumerate((near_own_ref, *near_refs)):
        for q in range(peers):
            @pl.when(lax.rem(place_ref[1] + k, peers) == q)
            def _(ref=ref, q=q):
                ref[...] = picked[block * q : block * q + block]


def gather(place, features, far_index, near_index, peers):
    width, dtype = features.shape[1], features.dtype
    far = jax.ShapeDtypeStruct((far_index.size, width), dtype)
    near = jax.ShapeDtypeStruct((near_index.size // peers, width), dtype)
    return pl.pallas_call(
        gather_kernel,
        out_shape=(far, far) + (near,) * peers,
        in_specs=[SMEM, VMEM, VMEM, VMEM],
        out_specs=(VMEM,) * (2 + peers),
        compiler_params=pltpu.CompilerParams(vmem_limit_bytes=24 * 2**20),
    )(place, features, far_index.reshape(-1, LANES), near_index.reshape(-1, LANES))


def layer_kernel(
    place_ref, dst_ref, inner_ref, outer_ref, live_ref, features_ref, far_ref, tile_ref, weight_ref, *rest
):
    *near_refs, hidden_ref, parts_ref, sum_ref, near_ref = rest
    peers = len(near_refs)
    block = near_ref.shape[0] // peers
    for k, ref in enumerate(near_refs):
        at = lax.rem(place_ref[1] + peers - k, peers)
        near_ref[pl.ds(pl.multiple_of(at * block, block), block), :] = ref[...]
    slots, tile = inner_ref.shape[0], tile_ref.shape[1]
    far_tiles = far_ref.shape[0] // tile
    sum_ref[...] = jnp.zeros_like(sum_ref)

    def add(c, source):
        to = pl.ds(pl.multiple_of(dst_ref[c] * tile, tile), tile)
        sum_ref[to, :] += contract(tile_ref[c], source, ((1,), (0,)))

    def rows_of(ref, index):
        return ref[pl.ds(pl.multiple_of(index * tile, tile), tile), :]

    for k in range(slots):
        @pl.when(k < live_ref[0, 0])
        def _(k=k):
            add(k, rows_of(features_ref, inner_ref[k]))

        @pl.when((k < live_ref[0, 1]) & (outer_ref[k] < far_tiles))
        def _(k=k):
            add(slots + k, rows_of(far_ref, outer_ref[k]))

        @pl.when((k < live_ref[0, 1]) & (outer_ref[k] >= far_tiles))
        def _(k=k):
            add(slots + k, rows_of(near_ref, outer_ref[k] - far_tiles))

    projected = contract(sum_ref[...].astype(jnp.bfloat16), weight_ref[...], ((1,), (0,)))
    features = features_ref[...]
    wide = features.astype(jnp.float32)
    hidden = (wide + projected / (1.0 + jnp.exp(-projected))).astype(jnp.bfloat16)
    hidden_ref[...] = hidden
    gram = contract(hidden, hidden, ((0,), (0,)))
    cross = contract(hidden, features, ((0,), (0,)))
    first = 0
    for part in pack(gram, cross, jnp.sum(wide * wide)):
        parts_ref[first : first + part.shape[0], :] = part
        first += part.shape[0]


def layer(place, dst, inner, outer, live, features, far, tiles, weight, near):
    rows, width = features.shape
    near_rows = sum(n.shape[0] for n in near)
    return pl.pallas_call(
        layer_kernel,
        out_shape=(
            jax.ShapeDtypeStruct((rows, width), jnp.bfloat16),
            jax.ShapeDtypeStruct((2 * width + width // SUB, LANES), jnp.float32),
        ),
        in_specs=[SMEM] * 5 + [VMEM] * (4 + len(near)),
        out_specs=(VMEM, VMEM),
        scratch_shapes=[pltpu.VMEM((rows, width), jnp.float32), pltpu.VMEM((near_rows, width), features.dtype)],
        compiler_params=pltpu.CompilerParams(vmem_limit_bytes=32 * 2**20),
    )(place, dst, inner, outer, live, features, far, tiles, weight, *near)


def sum_over_all(parts):
    near, far = ("x", "c", "y"), "z"
    pieces = parts.reshape(lax.axis_size(near), 1, -1)
    own = jnp.sum(lax.all_to_all(pieces, near, 0, 0, tiled=True), 0)
    own = jnp.broadcast_to(own[None], (lax.axis_size(far), *own.shape))
    own = jnp.sum(lax.all_to_all(own, far, 0, 0, tiled=True), 0)
    own = jnp.broadcast_to(own[None], pieces.shape)
    return lax.all_to_all(own, near, 0, 0, tiled=True).reshape(parts.shape)


def body(
    features, weight, send_far, send_near, tile_dst, inner_src, outer_src, tile_live, tile_weight
):
    rows, width = features.shape
    core, y = lax.axis_index("c"), lax.axis_index("y")
    peers = lax.axis_size("y")
    place = jnp.stack([core, y]).astype(jnp.int32)
    far, turned, *near = gather(place, features, send_far, send_near, peers)
    crossed = lax.ppermute(turned, "c", [(0, 1), (1, 0)])
    upper = iota((1, SUB, 1), 1) >= SUB // 2
    mixed = jnp.where(upper == (core == 1), far.reshape(-1, SUB, width), crossed.reshape(-1, SUB, width))
    far = lax.all_to_all(mixed, ("x", "z"), 0, 0, tiled=True).reshape(-1, width)
    near = near[:1] + [
        lax.ppermute(near[k], "y", [(i, (i + k) % peers) for i in range(peers)]) for k in range(1, peers)
    ]
    hidden, parts = layer(
        place, tile_dst, inner_src, outer_src, tile_live, features, far, tile_weight, weight, near
    )
    parts = sum_over_all(parts)
    vertex_count = rows * lax.axis_size(DOM) * lax.axis_size("y")
    white, loss = whiten(parts, hidden, vertex_count)
    return white, loss[0, 0]


def solution(mesh):
    torus = Mesh(mesh.devices.reshape(4, 16, 2, mesh.shape["sub"]), MESH_AXES)
    whole = MESH_AXES
    return jax.shard_map(
        body,
        mesh=torus,
        in_specs=(
            P(whole, None), P(), P(whole), P(whole), P(whole), P(whole), P(whole), P(whole, None), P(whole, None, None),
        ),
        out_specs=(P(whole, None), P()),
        check_vma=False,
    )
```

```python
import functools

import jax
import jax.numpy as jnp
from jax import lax
from jax.experimental import pallas as pl
from jax.experimental.pallas import tpu as pltpu
from jax.sharding import Mesh
from jax.sharding import PartitionSpec as P

MESH_AXES = ("x", "z", "c", "y")
DOM = ("x", "z", "c")

EPSILON = 1e-05
PANEL = 32
SUB = 8
LANES = 128

VMEM = pl.BlockSpec(memory_space=pltpu.VMEM)
SMEM = pl.BlockSpec(memory_space=pltpu.SMEM)
HBM = pl.BlockSpec(memory_space=pltpu.HBM)


def iota(shape, dim):
    return lax.broadcasted_iota(jnp.int32, shape, dim)


def contract(a, b, dims, **kw):
    return lax.dot_general(a, b, (dims, ((), ())), preferred_element_type=jnp.float32, **kw)


def three_terms(x):
    high = x.astype(jnp.bfloat16)
    rest = x - high.astype(jnp.float32)
    middle = rest.astype(jnp.bfloat16)
    low = (rest - middle.astype(jnp.float32)).astype(jnp.bfloat16)
    return high, middle, low


def eliminate_panel(rows, near, first_lane, width):
    groups = PANEL // SUB
    rows, near = list(rows), list(near)
    lane = iota((SUB, width), 1)
    sub = iota((SUB, width), 0)
    sub_lane = iota((SUB, LANES), 0)
    pivots = [None] * groups
    full = (SUB, LANES)
    for b in range(groups):
        start = first_lane + SUB * b
        in_block = (lane >= start) & (lane < start + SUB)
        unit = jnp.where(lane - start == sub, 1.0, 0.0)
        rows[b] = jnp.where(in_block, unit, rows[b])
        for g in range(b + 1, groups):
            rows[g] = jnp.where(in_block, 0.0, rows[g])
        column = [
            {g: jnp.take_along_axis(near[g], jnp.full(full, SUB * b + k, jnp.int32), 1, mode='promise_in_bounds') for g in range(b, groups)}
            for k in range(SUB)
        ]
        entry = {
            (m, k): jnp.broadcast_to(column[k][b][m : m + 1, :], full) for k in range(SUB) for m in range(k, SUB)
        }
        pivot = jnp.ones(full, jnp.float32)
        for k in range(0, SUB, 2):
            p, side, q = entry[k, k], entry[k + 1, k], entry[k + 1, k + 1]
            det = p * q - side * side
            inverse = pl.reciprocal(p)
            both = pl.reciprocal(p * det)
            second = both * p
            pivot = jnp.where(sub_lane == k, p, jnp.where(sub_lane == k + 1, det * inverse, pivot))
            left = {m: entry[m, k] for m in range(k + 2, SUB)}
            right = {m: p * entry[m, k + 1] - side * entry[m, k] for m in range(k + 2, SUB)}
            for n in range(k + 2, SUB):
                for m in range(n, SUB):
                    entry[m, n] = (entry[m, n] - left[m] * left[n] * inverse) - right[m] * right[n] * both
            first_scale, second_scale = {}, {}
            for g in range(b, groups):
                x, y = column[k][g], column[k + 1][g]
                first_scale[g] = x * inverse
                second_scale[g] = (p * y - side * x) * second
            first_scale[b] = jnp.where(sub_lane > k, first_scale[b], 0.0)
            second_scale[b] = jnp.where(sub_lane > k + 1, second_scale[b], 0.0)
            for m in range(k + 2, SUB):
                reduced = right[m] * inverse
                for g in range(b, groups):
                    column[m][g] = column[m][g] - first_scale[g] * left[m] - second_scale[g] * reduced
            ratio = side * inverse

            def lead_of(x):
                shape = (SUB, x.shape[1])
                first = jnp.broadcast_to(x[k : k + 1, :], shape)
                wide = jnp.concatenate([ratio] * (x.shape[1] // LANES), 1)
                return first, jnp.broadcast_to(x[k + 1 : k + 2, :], shape) - wide * first

            lead = lead_of(rows[b])
            lead_near = lead_of(near[b])
            for g in range(b, groups):
                one = jnp.concatenate([first_scale[g]] * (width // LANES), 1)
                two = jnp.concatenate([second_scale[g]] * (width // LANES), 1)
                rows[g] = rows[g] - one * lead[0] - two * lead[1]
                near[g] = near[g] - first_scale[g] * lead_near[0] - second_scale[g] * lead_near[1]
        pivots[b] = pivot
    return rows, pivots


def whiten_kernel(vertex_count, parts_ref, hidden_ref, white_ref, loss_ref, a_ref, v_ref):
    width = a_ref.shape[0]
    groups = PANEL // SUB
    packed = jnp.concatenate([parts_ref[:width, :], parts_ref[width : 2 * width, :]], 1)
    row, col = iota((width, width), 0), iota((width, width), 1)
    gram = jnp.where(row >= col, packed, packed.T)
    a_ref[...] = gram / vertex_count + jnp.where(row == col, EPSILON, 0.0)

    def panel(j, carry):
        first = pl.multiple_of(j * PANEL, PANEL)
        block = a_ref[pl.ds(first, PANEL), :]
        turned = pltpu.roll(block, lax.rem(width - first, width), 1)[:, :LANES]
        rows, pivots = eliminate_panel(
            [block[SUB * g : SUB * g + SUB] for g in range(groups)],
            [turned[SUB * g : SUB * g + SUB] for g in range(groups)],
            first,
            width,
        )
        whole = jnp.concatenate(rows, 0)
        pivot = jnp.concatenate(pivots, 0)
        pivot = jnp.concatenate([pivot] * (width // LANES), 1)
        lane = iota((PANEL, width), 1)
        lower = lane <= iota((PANEL, width), 0) + first
        v_ref[pl.ds(first, PANEL), :] = jnp.where(lower, whole * lax.rsqrt(pivot), 0.0)
        h, m, l = three_terms(whole / pivot)
        hh, mm, ll = three_terms(jnp.where(lower | (lane >= first + PANEL), whole, 0.0))
        update = contract(
            jnp.concatenate([h, h, m, h, l, m], 0), jnp.concatenate([hh, mm, hh, ll, hh, mm], 0), ((0,), (0,))
        )
        lanes = iota((width, width), 1)
        kept = jnp.where((lanes >= first) & (lanes < first + PANEL), 0.0, a_ref[...])
        a_ref[...] = kept - update
        return carry

    lax.fori_loop(0, width // PANEL, panel, 0, unroll=True)

    inverse = v_ref[...]
    high = inverse.astype(jnp.bfloat16)
    low = (inverse - high.astype(jnp.float32)).astype(jnp.bfloat16)
    hidden = hidden_ref[...]
    white_ref[...] = (contract(hidden, high, ((1,), (1,))) + contract(hidden, low, ((1,), (1,)))).astype(white_ref.dtype)

    packed = jnp.concatenate([parts_ref[:width, :], parts_ref[width : 2 * width, :]], 1)
    turned = packed.T
    gram = jnp.where(row >= col, packed, turned)
    cross = jnp.where(row > col, turned, 0.0)
    spare = parts_ref[2 * width :, :]
    square_sum = spare[0, LANES - 1]
    image = contract(inverse, gram, ((1,), (0,)), precision=lax.Precision.HIGHEST)
    diagonal = diagonal_of(inverse) * spare
    doubled = inverse * (image - 2.0 * cross)
    total = jnp.sum(doubled) - 2.0 * jnp.sum(diagonal) + square_sum
    loss_ref[0, 0] = total / (vertex_count * width)


def whiten(parts, hidden, vertex_count):
    rows, width = hidden.shape
    return pl.pallas_call(
        functools.partial(whiten_kernel, vertex_count),
        out_shape=(jax.ShapeDtypeStruct((rows, width), jnp.bfloat16), jax.ShapeDtypeStruct((1, 1), jnp.float32)),
        in_specs=[VMEM, VMEM],
        out_specs=(VMEM, SMEM),
        scratch_shapes=[pltpu.VMEM((width, width), jnp.float32), pltpu.VMEM((width, width), jnp.float32)],
        compiler_params=pltpu.CompilerParams(vmem_limit_bytes=24 * 2**20),
    )(parts, hidden)


def diagonal_of(square):
    width = square.shape[0]
    row, col = iota((width, width), 0), iota((width, width), 1)
    kept = jnp.where(row == col, square, 0.0)
    kept = jnp.where(row[:, :LANES] < LANES, kept[:, :LANES], kept[:, LANES:])
    return jnp.sum(kept.reshape(width // SUB, SUB, LANES), 1)


def pack(gram, cross, square_sum):
    width = gram.shape[0]
    row, col = iota((width, width), 0), iota((width, width), 1)
    both = jnp.where(row >= col, gram, cross)
    spare = diagonal_of(cross)
    corner = (iota(spare.shape, 0) == 0) & (iota(spare.shape, 1) == LANES - 1)
    return [both[:, :LANES], both[:, LANES:], jnp.where(corner, square_sum, spare)]


def gather_kernel(features_hbm, far_hbm, near_hbm, *rest):
    *outs, features_ref, far_index_ref, near_index_ref, far_ref, near_ref, in_sems, far_sems, near_sems = rest
    far_out, *near_outs = outs
    arrivals = [
        pltpu.make_async_copy(source, target, in_sems.at[i])
        for i, (source, target) in enumerate(
            ((far_hbm, far_index_ref), (near_hbm, near_index_ref), (features_hbm, features_ref))
        )
    ]
    for copy in arrivals:
        copy.start()
    source = features_ref.shape[0]
    lane = iota((LANES, LANES), 1)

    def picks_of(index):
        wanted = jnp.broadcast_to(index.astype(jnp.float32), (LANES, LANES)).T.astype(jnp.int32)
        picks = [
            jnp.where(wanted == lane + LANES * s, 1.0, 0.0).astype(jnp.bfloat16) for s in range(source // LANES)
        ]
        return jnp.concatenate(picks, 1)

    arrivals[0].wait()
    arrivals[1].wait()
    far_picks = [picks_of(far_index_ref[r : r + 1, :]) for r in range(far_index_ref.shape[0])]
    near_picks = picks_of(near_index_ref[...])
    arrivals[2].wait()
    features = features_ref[...]
    leaving = []
    for r, picks in enumerate(far_picks):
        here = pl.ds(LANES * r, LANES)
        far_ref[here, :] = contract(picks, features, ((1,), (0,))).astype(far_ref.dtype)
        leaving.append(pltpu.make_async_copy(far_ref.at[here], far_out.at[here], far_sems.at[r]))
        leaving[-1].start()
    near_ref[...] = contract(near_picks, features, ((1,), (0,))).astype(near_ref.dtype)
    peers = len(near_outs)
    block = LANES // peers
    y = lax.axis_index("y")
    for k, out in enumerate(near_outs):
        first = pl.multiple_of(lax.rem(y + k, peers) * block, block)
        leaving.append(pltpu.make_async_copy(near_ref.at[pl.ds(first, block)], out, near_sems.at[k]))
        leaving[-1].start()
    for copy in leaving:
        copy.wait()


def gather(features, far_index, near_index, peers):
    width, dtype = features.shape[1], features.dtype
    far = jax.ShapeDtypeStruct((far_index.size, width), dtype)
    near = jax.ShapeDtypeStruct((near_index.size // peers, width), dtype)
    far_index, near_index = far_index.reshape(-1, LANES), near_index.reshape(-1, LANES)
    return pl.pallas_call(
        gather_kernel,
        out_shape=(far,) + (near,) * peers,
        in_specs=[HBM] * 3,
        out_specs=(HBM,) * (1 + peers),
        scratch_shapes=[
            pltpu.VMEM(features.shape, dtype),
            pltpu.VMEM(far_index.shape, jnp.int32),
            pltpu.VMEM(near_index.shape, jnp.int32),
            pltpu.VMEM(far.shape, dtype),
            pltpu.VMEM((near_index.size, width), dtype),
            pltpu.SemaphoreType.DMA((3,)),
            pltpu.SemaphoreType.DMA((far_index.shape[0],)),
            pltpu.SemaphoreType.DMA((peers,)),
        ],
        compiler_params=pltpu.CompilerParams(vmem_limit_bytes=62 * 2**20),
    )(features, far_index, near_index)


def add_tile(sum_ref, dst_ref, slot, weights, source_ref, index):
    tile = weights.shape[0]
    to = pl.ds(pl.multiple_of(dst_ref[slot] * tile, tile), tile)
    source = source_ref[pl.ds(pl.multiple_of(index * tile, tile), tile), :]
    sum_ref[to, :] += contract(weights, source, ((1,), (0,)))


def inner_kernel(dst_ref, inner_ref, outer_ref, live_ref, features_ref, tile_ref, sum_ref, square_ref):
    sum_ref[...] = jnp.zeros_like(sum_ref)
    for k in range(inner_ref.shape[0]):
        @pl.when(k < live_ref[0, 0])
        def _(k=k):
            add_tile(sum_ref, dst_ref, k, tile_ref[k], features_ref, inner_ref[k])

    wide = features_ref[...].astype(jnp.float32)
    square = jnp.sum((wide * wide).reshape(-1, SUB, wide.shape[1]), 0)
    square_ref[...] = sum(square[:, i : i + LANES] for i in range(0, wide.shape[1], LANES))


def inner_sums(dst, inner, outer, live, features, tiles):
    rows, width = features.shape
    return pl.pallas_call(
        inner_kernel,
        out_shape=(
            jax.ShapeDtypeStruct((rows, width), jnp.float32),
            jax.ShapeDtypeStruct((SUB, LANES), jnp.float32),
        ),
        in_specs=[SMEM] * 4 + [VMEM] * 2,
        out_specs=(VMEM, VMEM),
        compiler_params=pltpu.CompilerParams(vmem_limit_bytes=16 * 2**20),
        cost_estimate=pl.CostEstimate(flops=10**8, bytes_accessed=2 * 10**6, transcendentals=0),
    )(dst, inner, outer, live, features, tiles)


def layer_kernel(
    dst_ref, outer_ref, live_ref, features_ref, own_ref, crossed_ref, tile_ref, weight_ref, inner_sum_ref,
    square_ref, *rest,
):
    *near_refs, hidden_ref, parts_ref, sum_ref, near_ref, far_ref = rest
    own, crossed = (
        ref[...].astype(jnp.float32).reshape(-1, SUB, ref.shape[1]) for ref in (own_ref, crossed_ref)
    )
    core = jnp.where(iota(own.shape, 1) >= SUB // 2, 1, 0)
    far = jnp.where(core == lax.axis_index("c"), own, pltpu.roll(crossed, SUB // 2, 1))
    far_ref[...] = far.reshape(far_ref.shape).astype(far_ref.dtype)
    peers = len(near_refs)
    block = near_ref.shape[0] // peers
    for k, ref in enumerate(near_refs):
        at = lax.rem(lax.axis_index("y") + peers - k, peers)
        near_ref[pl.ds(pl.multiple_of(at * block, block), block), :] = ref[...]
    slots, tile = outer_ref.shape[0], tile_ref.shape[1]
    far_tiles = far_ref.shape[0] // tile
    sum_ref[...] = inner_sum_ref[...]
    for k in range(slots):
        @pl.when((k < live_ref[0, 1]) & (outer_ref[k] < far_tiles))
        def _(k=k):
            add_tile(sum_ref, dst_ref, slots + k, tile_ref[slots + k], far_ref, outer_ref[k])

        @pl.when((k < live_ref[0, 1]) & (outer_ref[k] >= far_tiles))
        def _(k=k):
            add_tile(sum_ref, dst_ref, slots + k, tile_ref[slots + k], near_ref, outer_ref[k] - far_tiles)

    projected = contract(sum_ref[...].astype(jnp.bfloat16), weight_ref[...], ((1,), (0,)))
    features = features_ref[...]
    wide = features.astype(jnp.float32)
    hidden = (wide + projected / (1.0 + jnp.exp(-projected))).astype(jnp.bfloat16)
    hidden_ref[...] = hidden
    gram = contract(hidden, hidden, ((0,), (0,)))
    cross = contract(hidden, features, ((0,), (0,)))
    first = 0
    for part in pack(gram, cross, jnp.sum(square_ref[...])):
        parts_ref[first : first + part.shape[0], :] = part
        first += part.shape[0]


def layer(dst, outer, live, features, far, crossed, tiles, weight, inner, near):
    rows, width = features.shape
    near_rows = sum(n.shape[0] for n in near)
    return pl.pallas_call(
        layer_kernel,
        out_shape=(
            jax.ShapeDtypeStruct((rows, width), jnp.bfloat16),
            jax.ShapeDtypeStruct((2 * width + width // SUB, LANES), jnp.float32),
        ),
        in_specs=[SMEM] * 3 + [VMEM] * (7 + len(near)),
        out_specs=(VMEM, VMEM),
        scratch_shapes=[
            pltpu.VMEM((rows, width), jnp.float32),
            pltpu.VMEM((near_rows, width), features.dtype),
            pltpu.VMEM(far.shape, features.dtype),
        ],
        compiler_params=pltpu.CompilerParams(vmem_limit_bytes=24 * 2**20),
    )(dst, outer, live, features, far, crossed, tiles, weight, *inner, *near)


def sum_over_all(parts):
    near, far = ("x", "c", "y"), "z"
    pieces = parts.reshape(lax.axis_size(near), 1, -1)
    own = jnp.sum(lax.all_to_all(pieces, near, 0, 0, tiled=True), 0)
    own = jnp.broadcast_to(own[None], (lax.axis_size(far), *own.shape))
    own = jnp.sum(lax.all_to_all(own, far, 0, 0, tiled=True), 0)
    own = jnp.broadcast_to(own[None], pieces.shape)
    return lax.all_to_all(own, near, 0, 0, tiled=True).reshape(parts.shape)


def body(
    features, weight, send_far, send_near, tile_dst, inner_src, outer_src, tile_live, tile_weight
):
    rows, width = features.shape
    peers = lax.axis_size("y")
    far, *near = gather(features, send_far, send_near, peers)
    far = lax.all_to_all(far.reshape(-1, SUB, width), ("x", "z"), 0, 0, tiled=True).reshape(-1, width)
    near = near[:1] + [
        lax.ppermute(near[k], "y", [(i, (i + k) % peers) for i in range(peers)]) for k in range(1, peers)
    ]
    inner = inner_sums(tile_dst, inner_src, outer_src, tile_live, features, tile_weight)
    far, near, inner = lax.optimization_barrier((far, near, inner))
    crossed = lax.ppermute(far, "c", [(0, 1), (1, 0)])
    hidden, parts = layer(
        tile_dst, outer_src, tile_live, features, far, crossed, tile_weight, weight, inner, near
    )
    parts = sum_over_all(parts)
    vertex_count = rows * lax.axis_size(DOM) * lax.axis_size("y")
    white, loss = whiten(parts, hidden, vertex_count)
    return white, loss[0, 0]


def solution(mesh):
    torus = Mesh(mesh.devices.reshape(4, 16, 2, mesh.shape["sub"]), MESH_AXES)
    whole = MESH_AXES
    return jax.shard_map(
        body,
        mesh=torus,
        in_specs=(
            P(whole, None), P(), P(whole), P(whole), P(whole), P(whole), P(whole), P(whole, None), P(whole, None, None),
        ),
        out_specs=(P(whole, None), P()),
        check_vma=False,
    )
```

```python
import functools

import jax
import jax.numpy as jnp
from jax import lax
from jax.experimental import pallas as pl
from jax.experimental.pallas import tpu as pltpu
from jax.sharding import Mesh
from jax.sharding import PartitionSpec as P

MESH_AXES = ("x", "z", "c", "y")
DOM = ("x", "z", "c")

EPSILON = 1e-05
PANEL = 64
SUB = 8
LANES = 128

VMEM = pl.BlockSpec(memory_space=pltpu.VMEM)
SMEM = pl.BlockSpec(memory_space=pltpu.SMEM)
HBM = pl.BlockSpec(memory_space=pltpu.HBM)


def iota(shape, dim):
    return lax.broadcasted_iota(jnp.int32, shape, dim)


def contract(a, b, dims, **kw):
    return lax.dot_general(a, b, (dims, ((), ())), preferred_element_type=jnp.float32, **kw)


def three_terms(x):
    high = x.astype(jnp.bfloat16)
    rest = x - high.astype(jnp.float32)
    middle = rest.astype(jnp.bfloat16)
    low = (rest - middle.astype(jnp.float32)).astype(jnp.bfloat16)
    return high, middle, low


def eliminate_panel(rows, first_lane):
    rows = list(rows)
    groups, width = len(rows), rows[0].shape[1]
    lane = iota((SUB, width), 1)
    sub = iota((SUB, width), 0)
    sub_lane = iota((SUB, LANES), 0)
    pivots = [None] * groups
    full = (SUB, LANES)

    def widened(x):
        return jnp.concatenate([x] * (width // LANES), 1)

    for b in range(groups):
        start = first_lane + SUB * b
        part = slice(start // LANES * LANES, start // LANES * LANES + LANES)
        column = [
            {
                g: jnp.take_along_axis(
                    rows[g][:, part], jnp.full(full, start % LANES + k, jnp.int32), 1, mode="promise_in_bounds"
                )
                for g in range(b, groups)
            }
            for k in range(SUB)
        ]
        entry = {
            (m, k): jnp.broadcast_to(column[k][b][m : m + 1, :], full) for k in range(SUB) for m in range(k, SUB)
        }
        in_block = (lane >= start) & (lane < start + SUB)
        rows[b] = jnp.where(in_block, jnp.where(lane - start == sub, 1.0, 0.0), rows[b])
        for g in range(b + 1, groups):
            rows[g] = jnp.where(in_block, 0.0, rows[g])
        pivot = jnp.ones(full, jnp.float32)
        for k in range(0, SUB, 2):
            p, side, q = entry[k, k], entry[k + 1, k], entry[k + 1, k + 1]
            det = p * q - side * side
            inverse = pl.reciprocal(p)
            both = pl.reciprocal(p * det)
            second = both * p
            pivot = jnp.where(sub_lane == k, p, jnp.where(sub_lane == k + 1, det * inverse, pivot))
            left = {m: entry[m, k] for m in range(k + 2, SUB)}
            right = {m: p * entry[m, k + 1] - side * entry[m, k] for m in range(k + 2, SUB)}
            for n in range(k + 2, SUB):
                for m in range(n, SUB):
                    entry[m, n] = (entry[m, n] - left[m] * left[n] * inverse) - right[m] * right[n] * both
            first_scale, second_scale = {}, {}
            for g in range(b, groups):
                x, y = column[k][g], column[k + 1][g]
                first_scale[g] = x * inverse
                second_scale[g] = (p * y - side * x) * second
            first_scale[b] = jnp.where(sub_lane > k, first_scale[b], 0.0)
            second_scale[b] = jnp.where(sub_lane > k + 1, second_scale[b], 0.0)
            for m in range(k + 2, SUB):
                reduced = right[m] * inverse
                for g in range(b, groups):
                    column[m][g] = column[m][g] - first_scale[g] * left[m] - second_scale[g] * reduced
            lead = jnp.broadcast_to(rows[b][k : k + 1, :], (SUB, width))
            next_lead = jnp.broadcast_to(rows[b][k + 1 : k + 2, :], (SUB, width)) - widened(side * inverse) * lead
            for g in range(b, groups):
                rows[g] = rows[g] - widened(first_scale[g]) * lead - widened(second_scale[g]) * next_lead
        pivots[b] = pivot
    return rows, pivots


def whiten_kernel(vertex_count, parts_ref, hidden_ref, white_ref, loss_ref, a_ref, v_ref):
    width = a_ref.shape[0]
    packed = jnp.concatenate([parts_ref[:width, :], parts_ref[width : 2 * width, :]], 1)
    row, col = iota((width, width), 0), iota((width, width), 1)
    gram = jnp.where(row >= col, packed, packed.T)
    a_ref[...] = gram / vertex_count + jnp.where(row == col, EPSILON, 0.0)

    for first in range(0, width, PANEL):
        last = first + PANEL
        rows, pivots = eliminate_panel(
            [a_ref[i : i + SUB, :] for i in range(first, last, SUB)], first
        )
        whole = jnp.concatenate(rows, 0)
        pivot = jnp.concatenate(pivots, 0)
        pivot = jnp.concatenate([pivot] * (width // LANES), 1)
        lane = iota((PANEL, width), 1)
        lower = lane <= iota((PANEL, width), 0) + first
        v_ref[first:last, :] = jnp.where(lower, whole * lax.rsqrt(pivot), 0.0)
        if last == width:
            break
        below = last // LANES * LANES
        h, m, l = three_terms((whole / pivot)[:, below:])
        hh, mm, ll = three_terms(jnp.where(lower | (lane >= last), whole, 0.0))
        update = contract(
            jnp.concatenate([h, h, m, h], 0), jnp.concatenate([hh, mm, hh, ll], 0), ((0,), (0,))
        ) + contract(jnp.concatenate([l, m], 0), jnp.concatenate([hh, mm], 0), ((0,), (0,)))
        lanes = iota((width - below, width), 1)
        kept = jnp.where((lanes >= first) & (lanes < last), 0.0, a_ref[below:, :])
        a_ref[below:, :] = kept - update

    inverse = v_ref[...]
    high = inverse.astype(jnp.bfloat16)
    low = (inverse - high.astype(jnp.float32)).astype(jnp.bfloat16)
    hidden = hidden_ref[...]
    white_ref[...] = (contract(hidden, high, ((1,), (1,))) + contract(hidden, low, ((1,), (1,)))).astype(white_ref.dtype)

    packed = jnp.concatenate([parts_ref[:width, :], parts_ref[width : 2 * width, :]], 1)
    turned = packed.T
    gram = jnp.where(row >= col, packed, turned)
    cross = jnp.where(row > col, turned, 0.0)
    spare = parts_ref[2 * width :, :]
    square_sum = spare[0, LANES - 1]
    image = contract(inverse, gram, ((1,), (0,)), precision=lax.Precision.HIGHEST)
    diagonal = diagonal_of(inverse) * spare
    doubled = inverse * (image - 2.0 * cross)
    total = jnp.sum(doubled) - 2.0 * jnp.sum(diagonal) + square_sum
    loss_ref[0, 0] = total / (vertex_count * width)


def whiten(parts, hidden, vertex_count):
    rows, width = hidden.shape
    return pl.pallas_call(
        functools.partial(whiten_kernel, vertex_count),
        out_shape=(jax.ShapeDtypeStruct((rows, width), jnp.bfloat16), jax.ShapeDtypeStruct((1, 1), jnp.float32)),
        in_specs=[VMEM, VMEM],
        out_specs=(VMEM, SMEM),
        scratch_shapes=[pltpu.VMEM((width, width), jnp.float32), pltpu.VMEM((width, width), jnp.float32)],
        compiler_params=pltpu.CompilerParams(vmem_limit_bytes=24 * 2**20),
    )(parts, hidden)


def diagonal_of(square):
    width = square.shape[0]
    row, col = iota((width, width), 0), iota((width, width), 1)
    kept = jnp.where(row == col, square, 0.0)
    kept = jnp.where(row[:, :LANES] < LANES, kept[:, :LANES], kept[:, LANES:])
    return jnp.sum(kept.reshape(width // SUB, SUB, LANES), 1)


def pack(gram, cross, square_sum):
    width = gram.shape[0]
    row, col = iota((width, width), 0), iota((width, width), 1)
    both = jnp.where(row >= col, gram, cross)
    spare = diagonal_of(cross)
    corner = (iota(spare.shape, 0) == 0) & (iota(spare.shape, 1) == LANES - 1)
    return [both[:, :LANES], both[:, LANES:], jnp.where(corner, square_sum, spare)]


def gather_kernel(features_hbm, far_hbm, near_hbm, *rest):
    *outs, features_ref, far_index_ref, near_index_ref, far_ref, near_ref, in_sems, far_sems, near_sems = rest
    far_out, *near_outs = outs
    arrivals = [
        pltpu.make_async_copy(source, target, in_sems.at[i])
        for i, (source, target) in enumerate(
            ((far_hbm, far_index_ref), (near_hbm, near_index_ref), (features_hbm, features_ref))
        )
    ]
    for copy in arrivals:
        copy.start()
    source = features_ref.shape[0]
    lane = iota((LANES, LANES), 1)

    def picks_of(index):
        wanted = jnp.broadcast_to(index.astype(jnp.float32), (LANES, LANES)).T.astype(jnp.int32)
        picks = [
            jnp.where(wanted == lane + LANES * s, 1.0, 0.0).astype(jnp.bfloat16) for s in range(source // LANES)
        ]
        return jnp.concatenate(picks, 1)

    arrivals[0].wait()
    arrivals[1].wait()
    far_picks = [picks_of(far_index_ref[r : r + 1, :]) for r in range(far_index_ref.shape[0])]
    near_picks = picks_of(near_index_ref[...])
    arrivals[2].wait()
    features = features_ref[...]
    leaving = []
    for r, picks in enumerate(far_picks):
        here = pl.ds(LANES * r, LANES)
        far_ref[here, :] = contract(picks, features, ((1,), (0,))).astype(far_ref.dtype)
        leaving.append(pltpu.make_async_copy(far_ref.at[here], far_out.at[here], far_sems.at[r]))
        leaving[-1].start()
    near_ref[...] = contract(near_picks, features, ((1,), (0,))).astype(near_ref.dtype)
    peers = len(near_outs)
    block = LANES // peers
    y = lax.axis_index("y")
    for k, out in enumerate(near_outs):
        first = pl.multiple_of(lax.rem(y + k, peers) * block, block)
        leaving.append(pltpu.make_async_copy(near_ref.at[pl.ds(first, block)], out, near_sems.at[k]))
        leaving[-1].start()
    for copy in leaving:
        copy.wait()


def gather(features, far_index, near_index, peers):
    width, dtype = features.shape[1], features.dtype
    far = jax.ShapeDtypeStruct((far_index.size, width), dtype)
    near = jax.ShapeDtypeStruct((near_index.size // peers, width), dtype)
    far_index, near_index = far_index.reshape(-1, LANES), near_index.reshape(-1, LANES)
    return pl.pallas_call(
        gather_kernel,
        out_shape=(far,) + (near,) * peers,
        in_specs=[HBM] * 3,
        out_specs=(HBM,) * (1 + peers),
        scratch_shapes=[
            pltpu.VMEM(features.shape, dtype),
            pltpu.VMEM(far_index.shape, jnp.int32),
            pltpu.VMEM(near_index.shape, jnp.int32),
            pltpu.VMEM(far.shape, dtype),
            pltpu.VMEM((near_index.size, width), dtype),
            pltpu.SemaphoreType.DMA((3,)),
            pltpu.SemaphoreType.DMA((far_index.shape[0],)),
            pltpu.SemaphoreType.DMA((peers,)),
        ],
        compiler_params=pltpu.CompilerParams(vmem_limit_bytes=62 * 2**20),
    )(features, far_index, near_index)


def add_tile(sum_ref, dst_ref, slot, weights, source_ref, index):
    tile = weights.shape[0]
    to = pl.ds(pl.multiple_of(dst_ref[slot] * tile, tile), tile)
    source = source_ref[pl.ds(pl.multiple_of(index * tile, tile), tile), :]
    sum_ref[to, :] += contract(weights, source, ((1,), (0,)))


def inner_kernel(dst_ref, inner_ref, outer_ref, live_ref, features_ref, tile_ref, sum_ref, square_ref):
    sum_ref[...] = jnp.zeros_like(sum_ref)
    for k in range(inner_ref.shape[0]):
        @pl.when(k < live_ref[0, 0])
        def _(k=k):
            add_tile(sum_ref, dst_ref, k, tile_ref[k], features_ref, inner_ref[k])

    wide = features_ref[...].astype(jnp.float32)
    square = jnp.sum((wide * wide).reshape(-1, SUB, wide.shape[1]), 0)
    square_ref[...] = sum(square[:, i : i + LANES] for i in range(0, wide.shape[1], LANES))


def inner_sums(dst, inner, outer, live, features, tiles):
    rows, width = features.shape
    return pl.pallas_call(
        inner_kernel,
        out_shape=(
            jax.ShapeDtypeStruct((rows, width), jnp.float32),
            jax.ShapeDtypeStruct((SUB, LANES), jnp.float32),
        ),
        in_specs=[SMEM] * 4 + [VMEM] * 2,
        out_specs=(VMEM, VMEM),
        compiler_params=pltpu.CompilerParams(vmem_limit_bytes=16 * 2**20),
        cost_estimate=pl.CostEstimate(flops=10**8, bytes_accessed=2 * 10**6, transcendentals=0),
    )(dst, inner, outer, live, features, tiles)


def layer_kernel(
    dst_ref, outer_ref, live_ref, features_ref, own_ref, crossed_ref, tile_ref, weight_ref, inner_sum_ref, square_ref, *rest
):
    *near_refs, hidden_ref, parts_ref, sum_ref, table_ref = rest
    own, crossed = (
        ref[...].astype(jnp.float32).reshape(-1, SUB, ref.shape[1]) for ref in (own_ref, crossed_ref)
    )
    core = jnp.where(iota(own.shape, 1) >= SUB // 2, 1, 0)
    far = jnp.where(core == lax.axis_index("c"), own, pltpu.roll(crossed, SUB // 2, 1))
    far_rows = own_ref.shape[0]
    table_ref[:far_rows, :] = far.reshape(own_ref.shape).astype(table_ref.dtype)
    peers = len(near_refs)
    for k, ref in enumerate(near_refs):
        block = ref.shape[0]
        at = far_rows + lax.rem(lax.axis_index("y") + peers - k, peers) * block
        table_ref[pl.ds(pl.multiple_of(at, block), block), :] = ref[...]
    slots, tile = outer_ref.shape[0], tile_ref.shape[1]
    sum_ref[...] = inner_sum_ref[...]
    products = []
    for k in range(slots):
        source = table_ref[pl.ds(pl.multiple_of(outer_ref[k] * tile, tile), tile), :]
        product = contract(tile_ref[slots + k], source, ((1,), (0,)))
        products.append(jnp.where(k < live_ref[0, 1], product, 0.0))
    for k, product in enumerate(products):
        to = pl.ds(pl.multiple_of(dst_ref[slots + k] * tile, tile), tile)
        sum_ref[to, :] += product

    projected = contract(sum_ref[...].astype(jnp.bfloat16), weight_ref[...], ((1,), (0,)))
    features = features_ref[...]
    wide = features.astype(jnp.float32)
    hidden = (wide + projected / (1.0 + jnp.exp(-projected))).astype(jnp.bfloat16)
    hidden_ref[...] = hidden
    gram = contract(hidden, hidden, ((0,), (0,)))
    cross = contract(hidden, features, ((0,), (0,)))
    first = 0
    for part in pack(gram, cross, jnp.sum(square_ref[...])):
        parts_ref[first : first + part.shape[0], :] = part
        first += part.shape[0]


def layer(dst, outer, live, features, far, crossed, tiles, weight, inner, near):
    rows, width = features.shape
    near_rows = sum(n.shape[0] for n in near)
    return pl.pallas_call(
        layer_kernel,
        out_shape=(
            jax.ShapeDtypeStruct((rows, width), jnp.bfloat16),
            jax.ShapeDtypeStruct((2 * width + width // SUB, LANES), jnp.float32),
        ),
        in_specs=[SMEM] * 3 + [VMEM] * (7 + len(near)),
        out_specs=(VMEM, VMEM),
        scratch_shapes=[
            pltpu.VMEM((rows, width), jnp.float32),
            pltpu.VMEM((far.shape[0] + near_rows, width), features.dtype),
        ],
        compiler_params=pltpu.CompilerParams(vmem_limit_bytes=24 * 2**20),
    )(dst, outer, live, features, far, crossed, tiles, weight, *inner, *near)


def sum_over_all(parts):
    near, far = ("x", "c", "y"), "z"
    pieces = parts.reshape(lax.axis_size(near), 1, -1)
    own = jnp.sum(lax.all_to_all(pieces, near, 0, 0, tiled=True), 0)
    own = jnp.broadcast_to(own[None], (lax.axis_size(far), *own.shape))
    own = jnp.sum(lax.all_to_all(own, far, 0, 0, tiled=True), 0)
    own = jnp.broadcast_to(own[None], pieces.shape)
    return lax.all_to_all(own, near, 0, 0, tiled=True).reshape(parts.shape)


def body(
    features, weight, send_far, send_near, tile_dst, inner_src, outer_src, tile_live, tile_weight
):
    rows, width = features.shape
    peers = lax.axis_size("y")
    far, *near = gather(features, send_far, send_near, peers)
    far = lax.all_to_all(far.reshape(-1, SUB, width), ("x", "z"), 0, 0, tiled=True).reshape(-1, width)
    near = near[:1] + [
        lax.ppermute(near[k], "y", [(i, (i + k) % peers) for i in range(peers)]) for k in range(1, peers)
    ]
    inner = inner_sums(tile_dst, inner_src, outer_src, tile_live, features, tile_weight)
    far, near, inner = lax.optimization_barrier((far, near, inner))
    crossed = lax.ppermute(far, "c", [(0, 1), (1, 0)])
    hidden, parts = layer(
        tile_dst, outer_src, tile_live, features, far, crossed, tile_weight, weight, inner, near
    )
    parts = sum_over_all(parts)
    vertex_count = rows * lax.axis_size(DOM) * lax.axis_size("y")
    white, loss = whiten(parts, hidden, vertex_count)
    return white, loss[0, 0]


def solution(mesh):
    torus = Mesh(mesh.devices.reshape(4, 16, 2, mesh.shape["sub"]), MESH_AXES)
    whole = MESH_AXES
    return jax.shard_map(
        body,
        mesh=torus,
        in_specs=(
            P(whole, None), P(), P(whole), P(whole), P(whole), P(whole), P(whole), P(whole, None), P(whole, None, None),
        ),
        out_specs=(P(whole, None), P()),
        check_vma=False,
    )
```

```python
import functools

import jax
import jax.numpy as jnp
from jax import lax
from jax.experimental import pallas as pl
from jax.experimental.pallas import tpu as pltpu
from jax.sharding import Mesh
from jax.sharding import PartitionSpec as P

MESH_AXES = ("x", "z", "c", "y")
DOM = ("x", "z", "c")

EPSILON = 1e-05
PANEL = 64
SUB = 8
LANES = 128

VMEM = pl.BlockSpec(memory_space=pltpu.VMEM)
SMEM = pl.BlockSpec(memory_space=pltpu.SMEM)
HBM = pl.BlockSpec(memory_space=pltpu.HBM)


def iota(shape, dim):
    return lax.broadcasted_iota(jnp.int32, shape, dim)


def contract(a, b, dims, **kw):
    return lax.dot_general(a, b, (dims, ((), ())), preferred_element_type=jnp.float32, **kw)


def three_terms(x):
    high = x.astype(jnp.bfloat16)
    rest = x - high.astype(jnp.float32)
    middle = rest.astype(jnp.bfloat16)
    low = (rest - middle.astype(jnp.float32)).astype(jnp.bfloat16)
    return high, middle, low


def eliminate_panel(rows, first_lane):
    rows = list(rows)
    groups, width = len(rows), rows[0].shape[1]
    lane = iota((SUB, width), 1)
    sub = iota((SUB, width), 0)
    sub_lane = iota((SUB, LANES), 0)
    pivots = [None] * groups
    full = (SUB, LANES)

    def widened(x):
        return jnp.concatenate([x] * (width // LANES), 1)

    def columns_of(b):
        start = first_lane + SUB * b
        part = slice(start // LANES * LANES, start // LANES * LANES + LANES)
        return [
            {
                g: jnp.take_along_axis(
                    rows[g][:, part], jnp.full(full, start % LANES + k, jnp.int32), 1, mode="promise_in_bounds"
                )
                for g in range(b, groups)
            }
            for k in range(SUB)
        ]

    ahead = []
    for b in range(groups):
        start = first_lane + SUB * b
        column = ahead if ahead else columns_of(b)
        ahead = columns_of(b + 1) if 0 < groups - b - 1 <= 3 else []
        entry = {
            (m, k): jnp.broadcast_to(column[k][b][m : m + 1, :], full) for k in range(SUB) for m in range(k, SUB)
        }
        in_block = (lane >= start) & (lane < start + SUB)
        rows[b] = jnp.where(in_block, jnp.where(lane - start == sub, 1.0, 0.0), rows[b])
        for g in range(b + 1, groups):
            rows[g] = jnp.where(in_block, 0.0, rows[g])
        pivot = jnp.ones(full, jnp.float32)
        for k in range(0, SUB, 2):
            p, side, q = entry[k, k], entry[k + 1, k], entry[k + 1, k + 1]
            det = p * q - side * side
            inverse = pl.reciprocal(p)
            both = pl.reciprocal(p * det)
            second = both * p
            pivot = jnp.where(sub_lane == k, p, jnp.where(sub_lane == k + 1, det * inverse, pivot))
            left = {m: entry[m, k] for m in range(k + 2, SUB)}
            right = {m: p * entry[m, k + 1] - side * entry[m, k] for m in range(k + 2, SUB)}
            for n in range(k + 2, SUB):
                for m in range(n, SUB):
                    entry[m, n] = (entry[m, n] - left[m] * left[n] * inverse) - right[m] * right[n] * both
            first_scale, second_scale = {}, {}
            for g in range(b, groups):
                x, y = column[k][g], column[k + 1][g]
                below = p * y - side * x
                first_scale[g] = x * inverse
                second_scale[g] = below * second
                if ahead and g == b + 1:
                    next_left, next_right = x, below * inverse
            for m in range(SUB if ahead else 0):
                one = jnp.broadcast_to(next_left[m : m + 1, :], full)
                two = jnp.broadcast_to(next_right[m : m + 1, :], full)
                for g in range(b + 1, groups):
                    ahead[m][g] = ahead[m][g] - first_scale[g] * one - second_scale[g] * two
            first_scale[b] = jnp.where(sub_lane > k, first_scale[b], 0.0)
            second_scale[b] = jnp.where(sub_lane > k + 1, second_scale[b], 0.0)
            for m in range(k + 2, SUB):
                reduced = right[m] * inverse
                for g in range(b, groups):
                    column[m][g] = column[m][g] - first_scale[g] * left[m] - second_scale[g] * reduced
            lead = jnp.broadcast_to(rows[b][k : k + 1, :], (SUB, width))
            next_lead = jnp.broadcast_to(rows[b][k + 1 : k + 2, :], (SUB, width)) - widened(side * inverse) * lead
            for g in range(b, groups):
                rows[g] = rows[g] - widened(first_scale[g]) * lead - widened(second_scale[g]) * next_lead
        pivots[b] = pivot
    return rows, pivots


def whiten_kernel(vertex_count, parts_ref, hidden_ref, white_ref, loss_ref, a_ref, v_ref):
    width = a_ref.shape[0]
    packed = jnp.concatenate([parts_ref[:width, :], parts_ref[width : 2 * width, :]], 1)
    row, col = iota((width, width), 0), iota((width, width), 1)
    gram = jnp.where(row >= col, packed, packed.T)
    a_ref[...] = gram / vertex_count + jnp.where(row == col, EPSILON, 0.0)

    for first in range(0, width, PANEL):
        last = first + PANEL
        rows, pivots = eliminate_panel(
            [a_ref[i : i + SUB, :] for i in range(first, last, SUB)], first
        )
        whole = jnp.concatenate(rows, 0)
        pivot = jnp.concatenate(pivots, 0)
        pivot = jnp.concatenate([pivot] * (width // LANES), 1)
        lane = iota((PANEL, width), 1)
        lower = lane <= iota((PANEL, width), 0) + first
        v_ref[first:last, :] = jnp.where(lower, whole * lax.rsqrt(pivot), 0.0)
        if last == width:
            break
        below = last // LANES * LANES
        h, m, l = three_terms((whole / pivot)[:, below:])
        hh, mm, ll = three_terms(jnp.where(lower | (lane >= last), whole, 0.0))
        update = contract(
            jnp.concatenate([h, h, m, h], 0), jnp.concatenate([hh, mm, hh, ll], 0), ((0,), (0,))
        ) + contract(jnp.concatenate([l, m], 0), jnp.concatenate([hh, mm], 0), ((0,), (0,)))
        lanes = iota((width - below, width), 1)
        kept = jnp.where((lanes >= first) & (lanes < last), 0.0, a_ref[below:, :])
        a_ref[below:, :] = kept - update

    inverse = v_ref[...]
    high = inverse.astype(jnp.bfloat16)
    low = (inverse - high.astype(jnp.float32)).astype(jnp.bfloat16)
    hidden = hidden_ref[...]
    white_ref[...] = (contract(hidden, high, ((1,), (1,))) + contract(hidden, low, ((1,), (1,)))).astype(white_ref.dtype)

    packed = jnp.concatenate([parts_ref[:width, :], parts_ref[width : 2 * width, :]], 1)
    turned = packed.T
    gram = jnp.where(row >= col, packed, turned)
    cross = jnp.where(row > col, turned, 0.0)
    spare = parts_ref[2 * width :, :]
    square_sum = spare[0, LANES - 1]
    image = contract(inverse, gram, ((1,), (0,)), precision=lax.Precision.HIGHEST)
    diagonal = diagonal_of(inverse) * spare
    doubled = inverse * (image - 2.0 * cross)
    total = jnp.sum(doubled) - 2.0 * jnp.sum(diagonal) + square_sum
    loss_ref[0, 0] = total / (vertex_count * width)


def whiten(parts, hidden, vertex_count):
    rows, width = hidden.shape
    return pl.pallas_call(
        functools.partial(whiten_kernel, vertex_count),
        out_shape=(jax.ShapeDtypeStruct((rows, width), jnp.bfloat16), jax.ShapeDtypeStruct((1, 1), jnp.float32)),
        in_specs=[VMEM, VMEM],
        out_specs=(VMEM, SMEM),
        scratch_shapes=[pltpu.VMEM((width, width), jnp.float32), pltpu.VMEM((width, width), jnp.float32)],
        compiler_params=pltpu.CompilerParams(vmem_limit_bytes=24 * 2**20),
    )(parts, hidden)


def diagonal_of(square):
    width = square.shape[0]
    row, col = iota((width, width), 0), iota((width, width), 1)
    kept = jnp.where(row == col, square, 0.0)
    kept = jnp.where(row[:, :LANES] < LANES, kept[:, :LANES], kept[:, LANES:])
    return jnp.sum(kept.reshape(width // SUB, SUB, LANES), 1)


def pack(gram, cross, square_sum):
    width = gram.shape[0]
    row, col = iota((width, width), 0), iota((width, width), 1)
    both = jnp.where(row >= col, gram, cross)
    spare = diagonal_of(cross)
    corner = (iota(spare.shape, 0) == 0) & (iota(spare.shape, 1) == LANES - 1)
    return [both[:, :LANES], both[:, LANES:], jnp.where(corner, square_sum, spare)]


def gather_kernel(features_hbm, far_hbm, near_hbm, *rest):
    *outs, features_ref, far_index_ref, near_index_ref, far_ref, near_ref, in_sems, far_sems, near_sems = rest
    far_out, *near_outs = outs
    arrivals = [
        pltpu.make_async_copy(source, target, in_sems.at[i])
        for i, (source, target) in enumerate(
            ((far_hbm, far_index_ref), (near_hbm, near_index_ref), (features_hbm, features_ref))
        )
    ]
    for copy in arrivals:
        copy.start()
    source = features_ref.shape[0]
    lane = iota((LANES, LANES), 1)

    def picks_of(index):
        wanted = jnp.broadcast_to(index.astype(jnp.float32), (LANES, LANES)).T.astype(jnp.int32)
        picks = [
            jnp.where(wanted == lane + LANES * s, 1.0, 0.0).astype(jnp.bfloat16) for s in range(source // LANES)
        ]
        return jnp.concatenate(picks, 1)

    arrivals[0].wait()
    arrivals[1].wait()
    far_picks = [picks_of(far_index_ref[r : r + 1, :]) for r in range(far_index_ref.shape[0])]
    near_picks = picks_of(near_index_ref[...])
    arrivals[2].wait()
    features = features_ref[...]
    leaving = []
    for r, picks in enumerate(far_picks):
        here = pl.ds(LANES * r, LANES)
        far_ref[here, :] = contract(picks, features, ((1,), (0,))).astype(far_ref.dtype)
        leaving.append(pltpu.make_async_copy(far_ref.at[here], far_out.at[here], far_sems.at[r]))
        leaving[-1].start()
    near_ref[...] = contract(near_picks, features, ((1,), (0,))).astype(near_ref.dtype)
    peers = len(near_outs)
    block = LANES // peers
    y = lax.axis_index("y")
    for k, out in enumerate(near_outs):
        first = pl.multiple_of(lax.rem(y + k, peers) * block, block)
        leaving.append(pltpu.make_async_copy(near_ref.at[pl.ds(first, block)], out, near_sems.at[k]))
        leaving[-1].start()
    for copy in leaving:
        copy.wait()


def gather(features, far_index, near_index, peers):
    width, dtype = features.shape[1], features.dtype
    far = jax.ShapeDtypeStruct((far_index.size, width), dtype)
    near = jax.ShapeDtypeStruct((near_index.size // peers, width), dtype)
    far_index, near_index = far_index.reshape(-1, LANES), near_index.reshape(-1, LANES)
    return pl.pallas_call(
        gather_kernel,
        out_shape=(far,) + (near,) * peers,
        in_specs=[HBM] * 3,
        out_specs=(HBM,) * (1 + peers),
        scratch_shapes=[
            pltpu.VMEM(features.shape, dtype),
            pltpu.VMEM(far_index.shape, jnp.int32),
            pltpu.VMEM(near_index.shape, jnp.int32),
            pltpu.VMEM(far.shape, dtype),
            pltpu.VMEM((near_index.size, width), dtype),
            pltpu.SemaphoreType.DMA((3,)),
            pltpu.SemaphoreType.DMA((far_index.shape[0],)),
            pltpu.SemaphoreType.DMA((peers,)),
        ],
        compiler_params=pltpu.CompilerParams(vmem_limit_bytes=62 * 2**20),
    )(features, far_index, near_index)


def add_tile(sum_ref, dst_ref, slot, weights, source_ref, index):
    tile = weights.shape[0]
    to = pl.ds(pl.multiple_of(dst_ref[slot] * tile, tile), tile)
    source = source_ref[pl.ds(pl.multiple_of(index * tile, tile), tile), :]
    sum_ref[to, :] += contract(weights, source, ((1,), (0,)))


def inner_kernel(dst_ref, inner_ref, outer_ref, live_ref, features_ref, tile_ref, sum_ref, square_ref):
    sum_ref[...] = jnp.zeros_like(sum_ref)
    for k in range(inner_ref.shape[0]):
        @pl.when(k < live_ref[0, 0])
        def _(k=k):
            add_tile(sum_ref, dst_ref, k, tile_ref[k], features_ref, inner_ref[k])

    wide = features_ref[...].astype(jnp.float32)
    square = jnp.sum((wide * wide).reshape(-1, SUB, wide.shape[1]), 0)
    square_ref[...] = sum(square[:, i : i + LANES] for i in range(0, wide.shape[1], LANES))


def inner_sums(dst, inner, outer, live, features, tiles):
    rows, width = features.shape
    return pl.pallas_call(
        inner_kernel,
        out_shape=(
            jax.ShapeDtypeStruct((rows, width), jnp.float32),
            jax.ShapeDtypeStruct((SUB, LANES), jnp.float32),
        ),
        in_specs=[SMEM] * 4 + [VMEM] * 2,
        out_specs=(VMEM, VMEM),
        compiler_params=pltpu.CompilerParams(vmem_limit_bytes=16 * 2**20),
        cost_estimate=pl.CostEstimate(flops=10**8, bytes_accessed=2 * 10**6, transcendentals=0),
    )(dst, inner, outer, live, features, tiles)


def layer_kernel(
    dst_ref, outer_ref, live_ref, features_ref, own_ref, crossed_ref, tile_ref, weight_ref, inner_sum_ref, square_ref, *rest
):
    *near_refs, hidden_ref, parts_ref, sum_ref, table_ref = rest
    own, crossed = (
        ref[...].astype(jnp.float32).reshape(-1, SUB, ref.shape[1]) for ref in (own_ref, crossed_ref)
    )
    core = jnp.where(iota(own.shape, 1) >= SUB // 2, 1, 0)
    far = jnp.where(core == lax.axis_index("c"), own, pltpu.roll(crossed, SUB // 2, 1))
    far_rows = own_ref.shape[0]
    table_ref[:far_rows, :] = far.reshape(own_ref.shape).astype(table_ref.dtype)
    peers = len(near_refs)
    for k, ref in enumerate(near_refs):
        block = ref.shape[0]
        at = far_rows + lax.rem(lax.axis_index("y") + peers - k, peers) * block
        table_ref[pl.ds(pl.multiple_of(at, block), block), :] = ref[...]
    slots, tile = outer_ref.shape[0], tile_ref.shape[1]
    sum_ref[...] = inner_sum_ref[...]
    products = []
    for k in range(slots):
        source = table_ref[pl.ds(pl.multiple_of(outer_ref[k] * tile, tile), tile), :]
        product = contract(tile_ref[slots + k], source, ((1,), (0,)))
        products.append(jnp.where(k < live_ref[0, 1], product, 0.0))
    for k, product in enumerate(products):
        to = pl.ds(pl.multiple_of(dst_ref[slots + k] * tile, tile), tile)
        sum_ref[to, :] += product

    projected = contract(sum_ref[...].astype(jnp.bfloat16), weight_ref[...], ((1,), (0,)))
    features = features_ref[...]
    wide = features.astype(jnp.float32)
    hidden = (wide + projected / (1.0 + jnp.exp(-projected))).astype(jnp.bfloat16)
    hidden_ref[...] = hidden
    gram = contract(hidden, hidden, ((0,), (0,)))
    cross = contract(hidden, features, ((0,), (0,)))
    first = 0
    for part in pack(gram, cross, jnp.sum(square_ref[...])):
        parts_ref[first : first + part.shape[0], :] = part
        first += part.shape[0]


def layer(dst, outer, live, features, far, crossed, tiles, weight, inner, near):
    rows, width = features.shape
    near_rows = sum(n.shape[0] for n in near)
    return pl.pallas_call(
        layer_kernel,
        out_shape=(
            jax.ShapeDtypeStruct((rows, width), jnp.bfloat16),
            jax.ShapeDtypeStruct((2 * width + width // SUB, LANES), jnp.float32),
        ),
        in_specs=[SMEM] * 3 + [VMEM] * (7 + len(near)),
        out_specs=(VMEM, VMEM),
        scratch_shapes=[
            pltpu.VMEM((rows, width), jnp.float32),
            pltpu.VMEM((far.shape[0] + near_rows, width), features.dtype),
        ],
        compiler_params=pltpu.CompilerParams(vmem_limit_bytes=24 * 2**20),
    )(dst, outer, live, features, far, crossed, tiles, weight, *inner, *near)


def sum_over_all(parts):
    near, far = ("x", "c", "y"), "z"
    pieces = parts.reshape(lax.axis_size(near), 1, -1)
    own = jnp.sum(lax.all_to_all(pieces, near, 0, 0, tiled=True), 0)
    own = jnp.broadcast_to(own[None], (lax.axis_size(far), *own.shape))
    own = jnp.sum(lax.all_to_all(own, far, 0, 0, tiled=True), 0)
    own = jnp.broadcast_to(own[None], pieces.shape)
    return lax.all_to_all(own, near, 0, 0, tiled=True).reshape(parts.shape)


def body(
    features, weight, send_far, send_near, tile_dst, inner_src, outer_src, tile_live, tile_weight
):
    rows, width = features.shape
    peers = lax.axis_size("y")
    far, *near = gather(features, send_far, send_near, peers)
    far = lax.all_to_all(far.reshape(-1, SUB, width), ("x", "z"), 0, 0, tiled=True).reshape(-1, width)
    near = near[:1] + [
        lax.ppermute(near[k], "y", [(i, (i + k) % peers) for i in range(peers)]) for k in range(1, peers)
    ]
    inner = inner_sums(tile_dst, inner_src, outer_src, tile_live, features, tile_weight)
    far, near, inner = lax.optimization_barrier((far, near, inner))
    crossed = lax.ppermute(far, "c", [(0, 1), (1, 0)])
    hidden, parts = layer(
        tile_dst, outer_src, tile_live, features, far, crossed, tile_weight, weight, inner, near
    )
    parts = sum_over_all(parts)
    vertex_count = rows * lax.axis_size(DOM) * lax.axis_size("y")
    white, loss = whiten(parts, hidden, vertex_count)
    return white, loss[0, 0]


def solution(mesh):
    torus = Mesh(mesh.devices.reshape(4, 16, 2, mesh.shape["sub"]), MESH_AXES)
    whole = MESH_AXES
    return jax.shard_map(
        body,
        mesh=torus,
        in_specs=(
            P(whole, None), P(), P(whole), P(whole), P(whole), P(whole), P(whole), P(whole, None), P(whole, None, None),
        ),
        out_specs=(P(whole, None), P()),
        check_vma=False,
    )
```

```python
import functools

import jax
import jax.numpy as jnp
from jax import lax
from jax.experimental import pallas as pl
from jax.experimental.pallas import tpu as pltpu
from jax.sharding import Mesh
from jax.sharding import PartitionSpec as P

MESH_AXES = ("x", "z", "c", "y")
DOM = ("x", "z", "c")

EPSILON = 1e-05
PANEL = 64
SUB = 8
LANES = 128

VMEM = pl.BlockSpec(memory_space=pltpu.VMEM)
SMEM = pl.BlockSpec(memory_space=pltpu.SMEM)
HBM = pl.BlockSpec(memory_space=pltpu.HBM)


def iota(shape, dim):
    return lax.broadcasted_iota(jnp.int32, shape, dim)


def contract(a, b, dims, **kw):
    return lax.dot_general(a, b, (dims, ((), ())), preferred_element_type=jnp.float32, **kw)


def three_terms(x):
    high = x.astype(jnp.bfloat16)
    rest = x - high.astype(jnp.float32)
    middle = rest.astype(jnp.bfloat16)
    low = (rest - middle.astype(jnp.float32)).astype(jnp.bfloat16)
    return high, middle, low


def eliminate_panel(rows, first_lane):
    rows = list(rows)
    groups, width = len(rows), rows[0].shape[1]
    lane = iota((SUB, width), 1)
    sub = iota((SUB, width), 0)
    sub_lane = iota((SUB, LANES), 0)
    pivots = [None] * groups
    full = (SUB, LANES)

    def widened(x):
        return jnp.concatenate([x] * (width // LANES), 1)

    for b in range(groups):
        start = first_lane + SUB * b
        part = slice(start // LANES * LANES, start // LANES * LANES + LANES)
        column = [
            {
                g: jnp.take_along_axis(
                    rows[g][:, part], jnp.full(full, start % LANES + k, jnp.int32), 1, mode="promise_in_bounds"
                )
                for g in range(b, groups)
            }
            for k in range(SUB)
        ]
        entry = {
            (m, k): jnp.broadcast_to(column[k][b][m : m + 1, :], full) for k in range(SUB) for m in range(k, SUB)
        }
        in_block = (lane >= start) & (lane < start + SUB)
        rows[b] = jnp.where(in_block, jnp.where(lane - start == sub, 1.0, 0.0), rows[b])
        for g in range(b + 1, groups):
            rows[g] = jnp.where(in_block, 0.0, rows[g])
        pivot = jnp.ones(full, jnp.float32)
        for k in range(0, SUB, 2):
            p, side, q = entry[k, k], entry[k + 1, k], entry[k + 1, k + 1]
            det = p * q - side * side
            inverse = pl.reciprocal(p)
            both = pl.reciprocal(p * det)
            second = both * p
            pivot = jnp.where(sub_lane == k, p, jnp.where(sub_lane == k + 1, det * inverse, pivot))
            left = {m: entry[m, k] for m in range(k + 2, SUB)}
            right = {m: p * entry[m, k + 1] - side * entry[m, k] for m in range(k + 2, SUB)}
            for n in range(k + 2, SUB):
                for m in range(n, SUB):
                    entry[m, n] = (entry[m, n] - left[m] * left[n] * inverse) - right[m] * right[n] * both
            first_scale, second_scale = {}, {}
            for g in range(b, groups):
                x, y = column[k][g], column[k + 1][g]
                first_scale[g] = x * inverse
                second_scale[g] = (p * y - side * x) * second
            first_scale[b] = jnp.where(sub_lane > k, first_scale[b], 0.0)
            second_scale[b] = jnp.where(sub_lane > k + 1, second_scale[b], 0.0)
            for m in range(k + 2, SUB):
                reduced = right[m] * inverse
                for g in range(b, groups):
                    column[m][g] = column[m][g] - first_scale[g] * left[m] - second_scale[g] * reduced
            lead = jnp.broadcast_to(rows[b][k : k + 1, :], (SUB, width))
            next_lead = jnp.broadcast_to(rows[b][k + 1 : k + 2, :], (SUB, width)) - widened(side * inverse) * lead
            for g in range(b, groups):
                rows[g] = rows[g] - widened(first_scale[g]) * lead - widened(second_scale[g]) * next_lead
        pivots[b] = pivot
    return rows, pivots


def whiten_kernel(vertex_count, parts_ref, hidden_ref, white_ref, loss_ref, a_ref, v_ref):
    width = a_ref.shape[0]
    packed = jnp.concatenate([parts_ref[:width, :], parts_ref[width : 2 * width, :]], 1)
    row, col = iota((width, width), 0), iota((width, width), 1)
    gram = jnp.where(row >= col, packed, packed.T)
    a_ref[...] = gram / vertex_count + jnp.where(row == col, EPSILON, 0.0)

    for first in range(0, width, PANEL):
        last = first + PANEL
        rows, pivots = eliminate_panel(
            [a_ref[i : i + SUB, :] for i in range(first, last, SUB)], first
        )
        whole = jnp.concatenate(rows, 0)
        pivot = jnp.concatenate(pivots, 0)
        pivot = jnp.concatenate([pivot] * (width // LANES), 1)
        lane = iota((PANEL, width), 1)
        lower = lane <= iota((PANEL, width), 0) + first
        v_ref[first:last, :] = jnp.where(lower, whole * lax.rsqrt(pivot), 0.0)
        if last == width:
            break
        below = last // LANES * LANES
        h, m, l = three_terms((whole / pivot)[:, below:])
        hh, mm, ll = three_terms(jnp.where(lower | (lane >= last), whole, 0.0))
        update = contract(
            jnp.concatenate([h, h, m, h], 0), jnp.concatenate([hh, mm, hh, ll], 0), ((0,), (0,))
        ) + contract(jnp.concatenate([l, m], 0), jnp.concatenate([hh, mm], 0), ((0,), (0,)))
        lanes = iota((width - below, width), 1)
        kept = jnp.where((lanes >= first) & (lanes < last), 0.0, a_ref[below:, :])
        a_ref[below:, :] = kept - update

    inverse = v_ref[...]
    high = inverse.astype(jnp.bfloat16)
    low = (inverse - high.astype(jnp.float32)).astype(jnp.bfloat16)
    hidden = hidden_ref[...]
    white_ref[...] = (contract(hidden, high, ((1,), (1,))) + contract(hidden, low, ((1,), (1,)))).astype(white_ref.dtype)

    packed = jnp.concatenate([parts_ref[:width, :], parts_ref[width : 2 * width, :]], 1)
    turned = packed.T
    gram = jnp.where(row >= col, packed, turned)
    cross = jnp.where(row > col, turned, 0.0)
    spare = parts_ref[2 * width :, :]
    square_sum = spare[0, LANES - 1]
    image = contract(inverse, gram, ((1,), (0,)), precision=lax.Precision.HIGHEST)
    diagonal = diagonal_of(inverse) * spare
    doubled = inverse * (image - 2.0 * cross)
    total = jnp.sum(doubled) - 2.0 * jnp.sum(diagonal) + square_sum
    loss_ref[0, 0] = total / (vertex_count * width)


def whiten(parts, hidden, vertex_count):
    rows, width = hidden.shape
    return pl.pallas_call(
        functools.partial(whiten_kernel, vertex_count),
        out_shape=(jax.ShapeDtypeStruct((rows, width), jnp.bfloat16), jax.ShapeDtypeStruct((1, 1), jnp.float32)),
        in_specs=[VMEM, VMEM],
        out_specs=(VMEM, SMEM),
        scratch_shapes=[pltpu.VMEM((width, width), jnp.float32), pltpu.VMEM((width, width), jnp.float32)],
        compiler_params=pltpu.CompilerParams(vmem_limit_bytes=24 * 2**20),
    )(parts, hidden)


def diagonal_of(square):
    width = square.shape[0]
    row, col = iota((width, width), 0), iota((width, width), 1)
    kept = jnp.where(row == col, square, 0.0)
    kept = jnp.where(row[:, :LANES] < LANES, kept[:, :LANES], kept[:, LANES:])
    return jnp.sum(kept.reshape(width // SUB, SUB, LANES), 1)


def pack(gram, cross, square_sum):
    width = gram.shape[0]
    row, col = iota((width, width), 0), iota((width, width), 1)
    both = jnp.where(row >= col, gram, cross)
    spare = diagonal_of(cross)
    corner = (iota(spare.shape, 0) == 0) & (iota(spare.shape, 1) == LANES - 1)
    return [both[:, :LANES], both[:, LANES:], jnp.where(corner, square_sum, spare)]


def gather_kernel(features_hbm, far_hbm, near_hbm, *rest):
    *outs, features_ref, far_index_ref, near_index_ref, far_ref, near_ref, in_sems, far_sems, near_sems = rest
    far_out, *near_outs = outs
    arrivals = [
        pltpu.make_async_copy(source, target, in_sems.at[i])
        for i, (source, target) in enumerate(
            ((far_hbm, far_index_ref), (near_hbm, near_index_ref), (features_hbm, features_ref))
        )
    ]
    for copy in arrivals:
        copy.start()
    source = features_ref.shape[0]
    lane = iota((LANES, LANES), 1)

    def picks_of(index):
        wanted = jnp.broadcast_to(index.astype(jnp.float32), (LANES, LANES)).T.astype(jnp.int32)
        picks = [
            jnp.where(wanted == lane + LANES * s, 1.0, 0.0).astype(jnp.bfloat16) for s in range(source // LANES)
        ]
        return jnp.concatenate(picks, 1)

    arrivals[0].wait()
    arrivals[1].wait()
    far_picks = [picks_of(far_index_ref[r : r + 1, :]) for r in range(far_index_ref.shape[0])]
    near_picks = picks_of(near_index_ref[...])
    arrivals[2].wait()
    features = features_ref[...]
    leaving = []
    for r, picks in enumerate(far_picks):
        here = pl.ds(LANES * r, LANES)
        far_ref[here, :] = contract(picks, features, ((1,), (0,))).astype(far_ref.dtype)
        leaving.append(pltpu.make_async_copy(far_ref.at[here], far_out.at[here], far_sems.at[r]))
        leaving[-1].start()
    near_ref[...] = contract(near_picks, features, ((1,), (0,))).astype(near_ref.dtype)
    peers = len(near_outs)
    block = LANES // peers
    y = lax.axis_index("y")
    for k, out in enumerate(near_outs):
        first = pl.multiple_of(lax.rem(y + k, peers) * block, block)
        leaving.append(pltpu.make_async_copy(near_ref.at[pl.ds(first, block)], out, near_sems.at[k]))
        leaving[-1].start()
    for copy in leaving:
        copy.wait()


def gather(features, far_index, near_index, peers):
    width, dtype = features.shape[1], features.dtype
    far = jax.ShapeDtypeStruct((far_index.size, width), dtype)
    near = jax.ShapeDtypeStruct((near_index.size // peers, width), dtype)
    far_index, near_index = far_index.reshape(-1, LANES), near_index.reshape(-1, LANES)
    return pl.pallas_call(
        gather_kernel,
        out_shape=(far,) + (near,) * peers,
        in_specs=[HBM] * 3,
        out_specs=(HBM,) * (1 + peers),
        scratch_shapes=[
            pltpu.VMEM(features.shape, dtype),
            pltpu.VMEM(far_index.shape, jnp.int32),
            pltpu.VMEM(near_index.shape, jnp.int32),
            pltpu.VMEM(far.shape, dtype),
            pltpu.VMEM((near_index.size, width), dtype),
            pltpu.SemaphoreType.DMA((3,)),
            pltpu.SemaphoreType.DMA((far_index.shape[0],)),
            pltpu.SemaphoreType.DMA((peers,)),
        ],
        compiler_params=pltpu.CompilerParams(vmem_limit_bytes=62 * 2**20),
    )(features, far_index, near_index)


def add_tile(sum_ref, dst_ref, slot, weights, source_ref, index):
    tile = weights.shape[0]
    to = pl.ds(pl.multiple_of(dst_ref[slot] * tile, tile), tile)
    source = source_ref[pl.ds(pl.multiple_of(index * tile, tile), tile), :]
    sum_ref[to, :] += contract(weights, source, ((1,), (0,)))


def inner_kernel(dst_ref, inner_ref, outer_ref, live_ref, features_ref, tile_ref, sum_ref, square_ref):
    sum_ref[...] = jnp.zeros_like(sum_ref)
    for k in range(inner_ref.shape[0]):
        @pl.when(k < live_ref[0, 0])
        def _(k=k):
            add_tile(sum_ref, dst_ref, k, tile_ref[k], features_ref, inner_ref[k])

    wide = features_ref[...].astype(jnp.float32)
    square = jnp.sum((wide * wide).reshape(-1, SUB, wide.shape[1]), 0)
    square_ref[...] = sum(square[:, i : i + LANES] for i in range(0, wide.shape[1], LANES))


def inner_sums(dst, inner, outer, live, features, tiles):
    rows, width = features.shape
    return pl.pallas_call(
        inner_kernel,
        out_shape=(
            jax.ShapeDtypeStruct((rows, width), jnp.float32),
            jax.ShapeDtypeStruct((SUB, LANES), jnp.float32),
        ),
        in_specs=[SMEM] * 4 + [VMEM] * 2,
        out_specs=(VMEM, VMEM),
        compiler_params=pltpu.CompilerParams(vmem_limit_bytes=16 * 2**20),
        cost_estimate=pl.CostEstimate(flops=10**8, bytes_accessed=2 * 10**6, transcendentals=0),
    )(dst, inner, outer, live, features, tiles)


def layer_kernel(
    dst_ref, outer_ref, live_ref, features_ref, own_ref, crossed_ref, tile_ref, weight_ref, inner_sum_ref, square_ref, *rest
):
    *near_refs, hidden_ref, parts_ref, sum_ref, table_ref = rest
    own, crossed = (
        ref[...].astype(jnp.float32).reshape(-1, SUB, ref.shape[1]) for ref in (own_ref, crossed_ref)
    )
    core = jnp.where(iota(own.shape, 1) >= SUB // 2, 1, 0)
    far = jnp.where(core == lax.axis_index("c"), own, pltpu.roll(crossed, SUB // 2, 1))
    far_rows = own_ref.shape[0]
    table_ref[:far_rows, :] = far.reshape(own_ref.shape).astype(table_ref.dtype)
    peers = len(near_refs)
    for k, ref in enumerate(near_refs):
        block = ref.shape[0]
        at = far_rows + lax.rem(lax.axis_index("y") + peers - k, peers) * block
        table_ref[pl.ds(pl.multiple_of(at, block), block), :] = ref[...]
    slots, tile = outer_ref.shape[0], tile_ref.shape[1]
    sum_ref[...] = inner_sum_ref[...]
    products = []
    for k in range(slots):
        source = table_ref[pl.ds(pl.multiple_of(outer_ref[k] * tile, tile), tile), :]
        product = contract(tile_ref[slots + k], source, ((1,), (0,)))
        products.append(jnp.where(k < live_ref[0, 1], product, 0.0))
    for k, product in enumerate(products):
        to = pl.ds(pl.multiple_of(dst_ref[slots + k] * tile, tile), tile)
        sum_ref[to, :] += product

    projected = contract(sum_ref[...].astype(jnp.bfloat16), weight_ref[...], ((1,), (0,)))
    features = features_ref[...]
    wide = features.astype(jnp.float32)
    hidden = (wide + projected / (1.0 + jnp.exp(-projected))).astype(jnp.bfloat16)
    hidden_ref[...] = hidden
    gram = contract(hidden, hidden, ((0,), (0,)))
    cross = contract(hidden, features, ((0,), (0,)))
    first = 0
    for part in pack(gram, cross, jnp.sum(square_ref[...])):
        parts_ref[first : first + part.shape[0], :] = part
        first += part.shape[0]


def layer(dst, outer, live, features, far, crossed, tiles, weight, inner, near):
    rows, width = features.shape
    near_rows = sum(n.shape[0] for n in near)
    return pl.pallas_call(
        layer_kernel,
        out_shape=(
            jax.ShapeDtypeStruct((rows, width), jnp.bfloat16),
            jax.ShapeDtypeStruct((2 * width + width // SUB, LANES), jnp.float32),
        ),
        in_specs=[SMEM] * 3 + [VMEM] * (7 + len(near)),
        out_specs=(VMEM, VMEM),
        scratch_shapes=[
            pltpu.VMEM((rows, width), jnp.float32),
            pltpu.VMEM((far.shape[0] + near_rows, width), features.dtype),
        ],
        compiler_params=pltpu.CompilerParams(vmem_limit_bytes=24 * 2**20),
    )(dst, outer, live, features, far, crossed, tiles, weight, *inner, *near)


def sum_over_all(parts):
    near, far = ("x", "c", "y"), "z"
    pieces = parts.reshape(lax.axis_size(near), 1, -1)
    own = jnp.sum(lax.all_to_all(pieces, near, 0, 0, tiled=True), 0)
    own = jnp.broadcast_to(own[None], (lax.axis_size(far), *own.shape))
    own = jnp.sum(lax.all_to_all(own, far, 0, 0, tiled=True), 0)
    own = jnp.broadcast_to(own[None], pieces.shape)
    return lax.all_to_all(own, near, 0, 0, tiled=True).reshape(parts.shape)


def body(
    features, weight, send_far, send_near, tile_dst, inner_src, outer_src, tile_live, tile_weight
):
    rows, width = features.shape
    peers = lax.axis_size("y")
    far, *near = gather(features, send_far, send_near, peers)
    far = lax.all_to_all(far.reshape(-1, SUB, width), ("x", "z"), 0, 0, tiled=True).reshape(-1, width)
    by_one, by_two = ([(i, (i + k) % peers) for i in range(peers)] for k in (1, 2))
    block = near[0].shape[0]
    first = lax.ppermute(jnp.concatenate([near[1], near[3]]), "y", by_one)
    second = lax.ppermute(jnp.concatenate([near[2], first[block:]]), "y", by_two)
    near = [near[0], first[:block], second[:block], second[block:]]
    inner = inner_sums(tile_dst, inner_src, outer_src, tile_live, features, tile_weight)
    far, near, inner = lax.optimization_barrier((far, near, inner))
    crossed = lax.ppermute(far, "c", [(0, 1), (1, 0)])
    hidden, parts = layer(
        tile_dst, outer_src, tile_live, features, far, crossed, tile_weight, weight, inner, near
    )
    parts = sum_over_all(parts)
    vertex_count = rows * lax.axis_size(DOM) * lax.axis_size("y")
    white, loss = whiten(parts, hidden, vertex_count)
    return white, loss[0, 0]


def solution(mesh):
    torus = Mesh(mesh.devices.reshape(4, 16, 2, mesh.shape["sub"]), MESH_AXES)
    whole = MESH_AXES
    return jax.shard_map(
        body,
        mesh=torus,
        in_specs=(
            P(whole, None), P(), P(whole), P(whole), P(whole), P(whole), P(whole), P(whole, None), P(whole, None, None),
        ),
        out_specs=(P(whole, None), P()),
        check_vma=False,
    )
```
